32 devices in a mesh: dp: 4 (over z), pipe: 2 (over core), tensor: 4 (over y, x).
Axes of the slice: x: 2, y: 2, z: 4, core: 2. Of those that a mesh axis runs over, the one named last changes fastest.
Arguments:
- tokens: bfloat16 [8, 64, 4096], P('dp', None, 'tensor'), may hold values from -8 to 8
- w_query: bfloat16 [2, 2, 4096, 4096], P(None, 'pipe', 'dp', 'tensor'), may hold values from -8 to 8
- w_key: bfloat16 [2, 2, 4096, 1024], P(None, 'pipe', 'dp', 'tensor'), may hold values from -1 to 1
- w_value: bfloat16 [2, 2, 4096, 1024], P(None, 'pipe', 'dp', 'tensor'), may hold values from -0.09375 to 0.09375
- w_out: bfloat16 [2, 2, 4096, 4096], P(None, 'pipe', 'tensor', 'dp'), may hold values from -0.09375 to 0.09375
- norm_gain: float32 [2, 2, 4096], P(None, 'pipe'), may hold values from 0.5 to 1.5
- boundary: int32 [8], P('dp'), may hold values from 1 to 63
- skip_offset: int32 [8], P('dp'), may hold values from 0 to 131008
- doc_lengths: int32 [8, 4], P('dp'), may hold values from 1 to 32, 64 in all within a row
- batch_order: int32 [4, 2], P('dp'), may hold values from 0 to 1, each once within a row
Outputs:
- final_state: bfloat16 [8, 64, 4096], P('dp', 'pipe', 'tensor')
The draws below stay inside these ranges and needn't reach their ends.
Inputs may be any that keep to these rules, and one draw needn't show every extreme that they name: `doc_lengths`: each row sums to 64. `batch_order`: each row is a permutation.
All inputs are finite; a program needn't handle non-finite values.
Results may differ from the reference program's by a relative error of at most 0.014.
Values may be sent and summed in bfloat16 or wider, within the bound.
No kernel may reach another device: no remote copies, remote signals or barrier semaphores. Data moves between devices by JAX's collectives and lax.ppermute only.
A program may use at most 192 MiB of HBM per device.

```python
import math
from functools import partial
import jax
import jax.numpy as jnp
import numpy as np
from jax import lax

D = 4096
HEADS = 32
KV_HEADS = 8
HEAD_DIM = 128
SEQ = 64
MICRO = 2
DOCS = 4
POSITIONS = 131072
SECTIONS = 2
BATCH = 8
N_DP = 4


def draw_tokens(key, part):
    random_part = jax.random.normal(jax.random.fold_in(key, 11), (BATCH, SEQ, D), jnp.float32)
    return jnp.clip(random_part, -6.0, 6.0).astype(jnp.bfloat16)


def draw_w_query(key, part):
    raw_draw = jax.random.normal(jax.random.fold_in(key, 21), (2, SECTIONS, D, HEADS, HEAD_DIM), jnp.float32)
    values = jnp.clip(raw_draw, -6.0, 6.0) / jnp.sqrt(jnp.float32(D))
    return values.reshape(2, SECTIONS, D, HEADS * HEAD_DIM).astype(jnp.bfloat16)


def draw_w_key(key, part):
    raw_draw = jax.random.normal(jax.random.fold_in(key, 31), (2, SECTIONS, D, KV_HEADS, HEAD_DIM), jnp.float32)
    values = jnp.clip(raw_draw, -6.0, 6.0) / jnp.sqrt(jnp.float32(D))
    values = jnp.clip(values, -1.0, 1.0)
    return values.reshape(2, SECTIONS, D, KV_HEADS * HEAD_DIM).astype(jnp.bfloat16)


def with_ends(array, stream_key, low, high):
    dims = array.shape
    index_at = [jax.random.randint(jax.random.fold_in(stream_key, axis), (), 0, dims[axis]) for axis in range(len(dims))]
    array = array.at[tuple(index_at)].set(low)
    longest = dims.index(max(dims))
    index_at[longest] = (index_at[longest] + 1) % dims[longest]
    return array.at[tuple(index_at)].set(high)


def shard_levels(stream_key, shape, pieces, least, largest):
    loudness = 1.0
    for position, shards_of in pieces:
        draws = jax.random.uniform(jax.random.fold_in(jax.random.fold_in(stream_key, 6), position), (shards_of,), jnp.float32, least / len(pieces), largest / len(pieces))
        loudness = loudness * jnp.repeat(jnp.exp(draws), shape[position] // shards_of).reshape((-1,) + (1,) * (len(shape) - 1 - position))
    return loudness


def split_up(amount, total, reach, skew):
    portions = [(1 << 20) // math.isqrt(standing ** skew) + 1 for standing in range(2, amount + 1)]
    spare, counts = total - reach - (amount - 1), [1] * (amount - 1)
    while spare > 0:
        free = [i for i in range(amount - 1) if counts[i] < reach]
        mass, left = sum([portions[i] for i in free]), spare
        for i in free:
            addition = min(reach - counts[i], max(1, left * portions[i] // mass), spare)
            counts[i] = counts[i] + addition
            spare = spare - addition
    return np.array([reach] + counts)


def uneven(own_key, number_of, total, limit, slope):
    if number_of == 2:
        one = jax.random.randint(own_key, (), max(1, total - limit), min(limit, total - 1) + 1)
        return jnp.stack([one, total - one])
    tallies = jnp.asarray(split_up(number_of, total, limit, slope), jnp.int32)
    pairs = (number_of - 1) // 2
    giver, sink = tallies[1:1 + 2 * pairs:2], tallies[2:2 + 2 * pairs:2]
    slack = jnp.minimum(giver - 1, limit - sink)
    passed = jax.random.randint(jax.random.fold_in(own_key, 1), (pairs,), 0, 1 << 20) % (slack + 1)
    tallies = tallies.at[1:1 + 2 * pairs:2].set(giver - passed).at[2:2 + 2 * pairs:2].set(sink + passed)
    return tallies[jax.random.permutation(jax.random.fold_in(own_key, 2), number_of)]


def centred(stream_key, shape, width, bound, split=(), held_as=jnp.bfloat16):
    factor_of = shard_levels(stream_key, shape, split, -0.22, 0.18) if split else 1.0
    entries = jax.random.normal(stream_key, shape, jnp.float32) * width * factor_of
    return jnp.minimum(jnp.maximum(entries, -bound), bound).astype(held_as)


def setup_inputs(seed: int = 0) -> dict:
    arg_keys = jax.random.split(jax.random.key(seed), 11)
    return {
        "tokens": draw_tokens(jax.random.fold_in(arg_keys[10], 71), 0),
        "w_query": draw_w_query(jax.random.fold_in(arg_keys[10], 71), 0),
        "w_key": draw_w_key(jax.random.fold_in(arg_keys[10], 71), 0),
        "w_value": centred(arg_keys[3], (2, SECTIONS, D, KV_HEADS * HEAD_DIM), D ** -0.5, 0.09375, ((1, 2), (2, 4), (3, 4))),
        "w_out": centred(arg_keys[4], (2, SECTIONS, HEADS * HEAD_DIM, D), (HEADS * HEAD_DIM) ** -0.5, 0.09375, ((1, 2), (2, 4), (3, 4))),
        "norm_gain": jnp.clip(1.0 + 0.1 * jax.random.normal(arg_keys[5], (2, SECTIONS, D), jnp.float32), 0.5, 1.5),
        "boundary": with_ends(jax.random.randint(arg_keys[6], (BATCH,), 1, SEQ), jax.random.fold_in(arg_keys[6], 1), 1, SEQ - 1).astype(jnp.int32),
        "skip_offset": with_ends(jax.random.randint(arg_keys[7], (BATCH,), 0, POSITIONS - SEQ + 1), jax.random.fold_in(arg_keys[7], 1), 0, POSITIONS - SEQ).astype(jnp.int32),
        "doc_lengths": jax.vmap(lambda own: uneven(own, DOCS, SEQ, SEQ // 2, 1))(jax.random.split(arg_keys[8], BATCH)).reshape((BATCH, DOCS)).astype(jnp.int32),
        "batch_order": jax.vmap(lambda own: jax.random.permutation(own, MICRO))(jax.random.split(arg_keys[9], N_DP)).reshape((N_DP, MICRO)).astype(jnp.int32),
    }


ROPE_THETA = 500000.0
NORM_EPSILON = 1e-05

def rope_angles(positions, head_dim):
    half_dim = head_dim // 2
    exponent = jnp.arange(half_dim, dtype=jnp.float32) * (2.0 / head_dim)
    frequency = jnp.float32(ROPE_THETA) ** (-exponent)
    return positions.astype(jnp.float32)[..., None] * frequency

def rotate(values, angles):
    half_dim = values.shape[-1] // 2
    first_half = values[..., :half_dim]
    second = values[..., half_dim:]
    cosine = jnp.cos(angles)[:, None, :]
    sine_part = jnp.sin(angles)[:, None, :]
    return jnp.concatenate([first_half * cosine - second * sine_part, second * cosine + first_half * sine_part], axis=-1)

def sample_layout(first_cut, offset, lengths, seq_len):
    places = jnp.arange(seq_len, dtype=jnp.int32)
    positions = jnp.where(places < first_cut, places, places + offset).astype(jnp.int32)
    doc_ends = jnp.cumsum(lengths).astype(jnp.int32)
    doc_ids = lax.optimization_barrier(jnp.sum((places[:, None] >= doc_ends[None, :]).astype(jnp.int32), axis=1))
    allowed = (doc_ids[:, None] == doc_ids[None, :]) & (places[None, :] <= places[:, None])
    return (positions, allowed)

def attend(normed, q_weight, k_weight, v_weight, angles, allowed):
    seq_len = normed.shape[0]
    q_heads = q_weight.shape[1] // HEAD_DIM
    kv_heads = k_weight.shape[1] // HEAD_DIM
    group_size = q_heads // kv_heads
    queries = jnp.dot(normed, q_weight, preferred_element_type=jnp.float32)
    key_vecs = jnp.dot(normed, k_weight, preferred_element_type=jnp.float32)
    value_vecs = jnp.dot(normed, v_weight, preferred_element_type=jnp.float32).astype(jnp.bfloat16)
    value_vecs = value_vecs.reshape(seq_len, kv_heads, HEAD_DIM)
    queries = rotate(queries.reshape(seq_len, q_heads, HEAD_DIM), angles).astype(jnp.bfloat16)
    queries = queries.reshape(seq_len, kv_heads, group_size, HEAD_DIM)
    key_vecs = rotate(key_vecs.reshape(seq_len, kv_heads, HEAD_DIM), angles).astype(jnp.bfloat16)
    scores = jnp.einsum('skgd,tkd->kgst', queries.astype(jnp.float32), key_vecs.astype(jnp.float32)) * HEAD_DIM ** (-0.5)
    scores = jnp.where(allowed[None, None], scores, -jnp.inf)
    row_max = lax.optimization_barrier(jnp.max(scores, axis=-1, keepdims=True))
    exp_scores = jnp.exp(scores - row_max)
    weights = (exp_scores / lax.optimization_barrier(jnp.sum(exp_scores, axis=-1, keepdims=True))).astype(jnp.bfloat16)
    mixed = jnp.einsum('kgst,tkd->skgd', weights.astype(jnp.float32), value_vecs.astype(jnp.float32))
    return mixed.reshape(seq_len, q_heads * HEAD_DIM)

def layer_step(stream, gain_row, q_weight, k_weight, v_weight, o_weight, angles, allowed):
    widened = stream.astype(jnp.float32)
    inv_rms = lax.rsqrt(lax.optimization_barrier(jnp.mean(widened * widened, axis=-1, keepdims=True)) + NORM_EPSILON)
    normed = (widened * inv_rms * gain_row).astype(jnp.bfloat16)
    mixed = attend(normed, q_weight, k_weight, v_weight, angles, allowed).astype(jnp.bfloat16)
    projected = jnp.dot(mixed, o_weight, preferred_element_type=jnp.float32)
    return (widened + projected).astype(jnp.bfloat16)

def chained(stacked):
    return jnp.concatenate([stacked[0], stacked[1][::-1]], axis=0)

def reference(tokens, w_query, w_key, w_value, w_out, norm_gain, boundary, skip_offset, doc_lengths, batch_order):
    row_index = (jnp.arange(N_DP, dtype=jnp.int32)[:, None] * MICRO + batch_order.astype(jnp.int32)).reshape(-1).astype(jnp.int32)
    stream = jnp.take(tokens, row_index, axis=0)
    positions, allowed = jax.vmap(partial(sample_layout, seq_len=SEQ))(jnp.take(boundary, row_index), jnp.take(skip_offset, row_index), jnp.take(doc_lengths, row_index, axis=0))
    angles = rope_angles(positions, HEAD_DIM)
    layers = (chained(norm_gain), chained(w_query), chained(w_key), chained(w_value), chained(w_out))

    def advance(current, layer_weights):
        gain_row, q_weight, k_weight, v_weight, o_weight = layer_weights

        def per_sample(sample_rows, sample_angles, sample_allowed):
            return layer_step(sample_rows, gain_row, q_weight, k_weight, v_weight, o_weight, sample_angles, sample_allowed)
        return (jax.vmap(per_sample)(current, angles, allowed), None)
    stream, unused = lax.scan(advance, stream, layers)
    return stream
```

```python
from functools import partial

import jax
import jax.numpy as jnp
from jax import lax
from jax.experimental import pallas as pl
from jax.experimental.pallas import tpu as pltpu
from jax.sharding import PartitionSpec as P

HEAD_DIM = 128
LANES = 128
ROPE_THETA = 500000.0
NORM_EPSILON = 1e-05
VMEM_BYTES = 40 * 1024 * 1024


def rope_angles(positions, head_dim):
    half_dim = head_dim // 2
    exponent = jnp.arange(half_dim, dtype=jnp.float32) * (2.0 / head_dim)
    frequency = jnp.float32(ROPE_THETA) ** (-exponent)
    return positions.astype(jnp.float32)[..., None] * frequency


def sample_layout(first_cut, offset, lengths, seq_len):
    places = jnp.arange(seq_len, dtype=jnp.int32)
    positions = jnp.where(places < first_cut, places, places + offset)
    doc_ends = jnp.cumsum(lengths)
    doc_ids = jnp.sum((places[:, None] >= doc_ends[None, :]).astype(jnp.int32), axis=1)
    allowed = (doc_ids[:, None] == doc_ids[None, :]) & (places[None, :] <= places[:, None])
    return (positions, allowed)


def in_vmem(count):
    return [pl.BlockSpec(memory_space=pltpu.VMEM)] * count


def column_tiles(width, tile):
    return [(at, min(tile, width - at)) for at in range(0, width, tile)]


def qkv_kernel(n_in, n_out, place, *refs):
    blocks, (gain, wq, wk, wv) = refs[:n_in], refs[n_in : n_in + 4]
    outs, (rows, stats) = refs[n_in + 4 : n_in + 4 + n_out], refs[n_in + 4 + n_out :]
    size = blocks[0].shape[0]
    scale = gain[...]
    for m, block in enumerate(blocks):
        at = pl.ds(pl.multiple_of(place[m] * size, size), size)
        wide = block[...].astype(jnp.float32)
        rows[at, :] = (wide * scale).astype(jnp.bfloat16)
        total = jnp.sum(wide * wide, axis=-1, keepdims=True)
        stats[at, :] = jnp.broadcast_to(total, (size, LANES))
    out_size = outs[0].shape[0]
    start = 0
    for weight in (wq, wk, wv):
        for at, width in column_tiles(weight.shape[1], 512):
            product = jnp.dot(rows[...], weight[:, at : at + width], preferred_element_type=jnp.float32)
            for m, out in enumerate(outs):
                piece = product[m * out_size : (m + 1) * out_size]
                out[:, start + at : start + at + width] = piece.astype(out.dtype)
        start += weight.shape[1]
    total = stats[...]
    high = total.astype(jnp.bfloat16).astype(jnp.float32)
    lane = lax.broadcasted_iota(jnp.int32, total.shape, 1)
    split = jnp.where(lane < LANES // 2, high, total - high)
    for m, out in enumerate(outs):
        out[:, start : start + LANES] = split[m * out_size : (m + 1) * out_size].astype(out.dtype)


def project_qkv(blocks, place, gain, wq, wk, wv, n_out):
    n_in = len(blocks)
    total = n_in * blocks[0].shape[0]
    depth = blocks[0].shape[1]
    columns = wq.shape[1] + wk.shape[1] + wv.shape[1] + LANES
    shapes = [
        jax.ShapeDtypeStruct((total // n_out, columns), jnp.float32 if m == 0 and n_out > 1 else jnp.bfloat16)
        for m in range(n_out)
    ]
    return pl.pallas_call(
        partial(qkv_kernel, n_in, n_out),
        out_shape=shapes,
        in_specs=[pl.BlockSpec(memory_space=pltpu.SMEM)] + in_vmem(n_in + 4),
        out_specs=in_vmem(n_out),
        scratch_shapes=[pltpu.VMEM((total, depth), jnp.bfloat16), pltpu.VMEM((total, LANES), jnp.float32)],
        compiler_params=pltpu.CompilerParams(vmem_limit_bytes=VMEM_BYTES),
        cost_estimate=pl.CostEstimate(
            flops=2 * total * depth * columns, bytes_accessed=2 * depth * columns, transcendentals=0
        ),
        name="project_qkv",
    )(place, *blocks, gain, wq, wk, wv)


def attention_kernel(n_in, q_heads, kv_heads, model_width, *refs):
    blocks, (cosine, sine, mask, out) = refs[:n_in], refs[n_in:]
    samples, seq = cosine.shape[0], cosine.shape[1]
    group = q_heads // kv_heads

    def summed(rows, at, width):
        value = blocks[0][rows, at : at + width].astype(jnp.float32)
        for block in blocks[1:]:
            value = value + block[rows, at : at + width].astype(jnp.float32)
        return value

    k_at = q_heads * HEAD_DIM
    v_at = k_at + kv_heads * HEAD_DIM
    s_at = v_at + kv_heads * HEAD_DIM
    for s in range(samples):
        rows = slice(s * seq, (s + 1) * seq)
        parts = summed(rows, s_at, LANES)
        squares = parts[:, :1] + parts[:, LANES // 2 : LANES // 2 + 1]
        inverse = lax.rsqrt(squares * (1.0 / model_width) + NORM_EPSILON)
        cos, sin, bias = cosine[s], sine[s], mask[s]

        def rotated(at):
            value = summed(rows, at, HEAD_DIM) * inverse
            turned = pltpu.roll(value, HEAD_DIM // 2, 1)
            return (value * cos + turned * sin).astype(jnp.bfloat16)

        bias_all = jnp.concatenate([bias] * group, axis=0)
        for kv in range(kv_heads):
            key = rotated(k_at + kv * HEAD_DIM)
            value = (summed(rows, v_at + kv * HEAD_DIM, HEAD_DIM) * inverse).astype(jnp.bfloat16)
            query = jnp.concatenate([rotated((kv * group + g) * HEAD_DIM) for g in range(group)], axis=0)
            scores = lax.dot_general(query, key, (((1,), (1,)), ((), ())), preferred_element_type=jnp.float32)
            scores = scores * HEAD_DIM ** (-0.5) + bias_all
            top = jnp.max(scores, axis=-1, keepdims=True)
            weights = jnp.exp(scores - top)
            weights = weights / jnp.sum(weights, axis=-1, keepdims=True)
            mixed = jnp.dot(weights.astype(jnp.bfloat16), value, preferred_element_type=jnp.float32)
            for g in range(group):
                at = (kv * group + g) * HEAD_DIM
                out[rows, at : at + HEAD_DIM] = mixed[g * seq : (g + 1) * seq].astype(out.dtype)


def attend(blocks, cosine, sine, mask, q_heads, kv_heads, model_width):
    rows = blocks[0].shape[0]
    return pl.pallas_call(
        partial(attention_kernel, len(blocks), q_heads, kv_heads, model_width),
        out_shape=jax.ShapeDtypeStruct((rows, q_heads * HEAD_DIM), jnp.bfloat16),
        in_specs=in_vmem(len(blocks) + 3),
        out_specs=pl.BlockSpec(memory_space=pltpu.VMEM),
        compiler_params=pltpu.CompilerParams(vmem_limit_bytes=VMEM_BYTES),
        cost_estimate=pl.CostEstimate(
            flops=4 * rows * rows * q_heads * HEAD_DIM,
            bytes_accessed=2 * len(blocks) * rows * blocks[0].shape[1],
            transcendentals=rows * rows * q_heads,
        ),
        name="attend",
    )(*blocks, cosine, sine, mask)


def out_kernel(n_in, n_out, place, *refs):
    blocks, weight = refs[:n_in], refs[n_in]
    outs, (rows,) = refs[n_in + 1 : n_in + 1 + n_out], refs[n_in + 1 + n_out :]
    size = blocks[0].shape[0]
    for m, block in enumerate(blocks):
        rows[pl.ds(pl.multiple_of(place[m] * size, size), size), :] = block[...]
    out_size = outs[0].shape[0]
    for at, width in column_tiles(weight.shape[1], 512):
        product = jnp.dot(rows[...], weight[:, at : at + width], preferred_element_type=jnp.float32)
        for m, out in enumerate(outs):
            out[:, at : at + width] = product[m * out_size : (m + 1) * out_size].astype(out.dtype)


def project_out(blocks, place, weight, n_out):
    n_in = len(blocks)
    total = n_in * blocks[0].shape[0]
    depth, columns = weight.shape
    shapes = [
        jax.ShapeDtypeStruct((total // n_out, columns), jnp.float32 if m == 0 and n_out > 1 else jnp.bfloat16)
        for m in range(n_out)
    ]
    return pl.pallas_call(
        partial(out_kernel, n_in, n_out),
        out_shape=shapes,
        in_specs=[pl.BlockSpec(memory_space=pltpu.SMEM)] + in_vmem(n_in + 1),
        out_specs=in_vmem(n_out),
        scratch_shapes=[pltpu.VMEM((total, depth), jnp.bfloat16)],
        compiler_params=pltpu.CompilerParams(vmem_limit_bytes=VMEM_BYTES),
        cost_estimate=pl.CostEstimate(
            flops=2 * total * depth * columns, bytes_accessed=2 * depth * columns, transcendentals=0
        ),
        name="project_out",
    )(place, *blocks, weight)


def swapped(value, axis, by):
    return lax.ppermute(value, axis, [(i, i ^ by) for i in range(lax.axis_size(axis))])


def gather_blocks(block, axis, peers):
    return [block] + [swapped(block, axis, m) for m in range(1, peers)]


def trade_blocks(blocks, axis):
    return [blocks[0]] + [swapped(blocks[m], axis, m) for m in range(1, len(blocks))]


def total_of(blocks):
    value = blocks[0].astype(jnp.float32)
    for block in blocks[1:]:
        value = value + block.astype(jnp.float32)
    return value


def per_device(
    tokens,
    w_query,
    w_key,
    w_value,
    w_out,
    norm_gain,
    boundary,
    skip_offset,
    doc_lengths,
    batch_order,
):
    replicas, sections, groups = lax.axis_size("dp"), lax.axis_size("pipe"), lax.axis_size("tensor")
    my_replica, my_section, my_group = lax.axis_index("dp"), lax.axis_index("pipe"), lax.axis_index("tensor")
    micro_count, seq_len, local_width = tokens.shape
    model_width = local_width * groups
    slots = micro_count // sections
    rows = slots * seq_len
    depth = w_query.shape[2]
    q_heads = w_query.shape[3] // HEAD_DIM
    kv_heads = w_key.shape[3] // HEAD_DIM
    paired = replicas == groups and replicas & (replicas - 1) == 0

    samples = lax.dynamic_slice_in_dim(batch_order[0], my_section * slots, slots, 0)
    stream = jnp.take(tokens, samples, axis=0).reshape(rows, local_width)

    gain_rows = lax.dynamic_slice_in_dim(norm_gain, my_replica * depth, depth, 2)
    if sections == 2:
        traded = [swapped(w, "pipe", 1) for w in (gain_rows, w_query, w_key, w_value, w_out)]

        def layer_weights(index, section):
            return [
                jnp.where(my_section == section, mine[index, 0], theirs[index, 0])
                for mine, theirs in zip((gain_rows, w_query, w_key, w_value, w_out), traded)
            ]
    else:
        gathered = [
            lax.all_gather(w, "pipe", axis=1, tiled=True) for w in (gain_rows, w_query, w_key, w_value, w_out)
        ]

        def layer_weights(index, section):
            return [w[index, section] for w in gathered]

    positions, allowed = jax.vmap(partial(sample_layout, seq_len=seq_len))(
        jnp.take(boundary, samples),
        jnp.take(skip_offset, samples),
        jnp.take(doc_lengths, samples, axis=0),
    )
    angles = rope_angles(positions, HEAD_DIM)
    cosine, sine = jnp.cos(angles), jnp.sin(angles)
    cosine = jnp.concatenate([cosine, cosine], axis=-1)
    sine = jnp.concatenate([-sine, sine], axis=-1)
    mask = jnp.where(allowed, 0.0, -jnp.inf).astype(jnp.float32)

    if paired:
        turn = [(i * groups + j, j * groups + i) for i in range(replicas) for j in range(groups)]
        mine = lax.ppermute(stream, ("dp", "tensor"), turn)
        blocks = gather_blocks(mine, "tensor", groups)
        place = jnp.arange(groups, dtype=jnp.int32) ^ my_replica ^ my_group
    else:
        wide = lax.all_gather(stream, "tensor", axis=1, tiled=True)
        whole = lax.all_to_all(wide, "dp", split_axis=1, concat_axis=0, tiled=True)
        share = whole.shape[0] // groups
        mine = lax.dynamic_slice_in_dim(whole, my_group * share, share, 0)
        blocks = [whole]
        place = jnp.zeros((1,), jnp.int32)

    layers = [(0, s) for s in range(sections)] + [(1, s) for s in reversed(range(sections))]
    for number, (index, section) in enumerate(layers):
        gain, wq, wk, wv, wo = layer_weights(index, section)
        if number and paired:
            blocks = gather_blocks(mine, "tensor", groups)
        elif number:
            blocks = [lax.all_gather(mine, "tensor", axis=0, tiled=True)]
        sums = project_qkv(blocks, place, gain[None], wq, wk, wv, replicas if paired else 1)
        if paired:
            sums = trade_blocks(sums, "dp")
        else:
            pieces = sums[0].reshape(replicas, rows, sums[0].shape[1])
            pieces = lax.all_to_all(pieces, "dp", split_axis=0, concat_axis=0)
            sums = [jnp.sum(pieces.astype(jnp.float32), axis=0)]
        mixed = attend(sums, cosine, sine, mask, q_heads, kv_heads, model_width)
        if paired:
            mixed = gather_blocks(mixed, "dp", replicas)
        else:
            mixed = [lax.all_gather(mixed, "dp", axis=0, tiled=True)]
        shares = project_out(mixed, place, wo, groups if paired else 1)
        if paired:
            shares = total_of(trade_blocks(shares, "tensor"))
        else:
            pieces = shares[0].reshape(groups, mine.shape[0], depth)
            pieces = lax.all_to_all(pieces, "tensor", split_axis=0, concat_axis=0)
            shares = jnp.sum(pieces.astype(jnp.float32), axis=0)
        mine = (mine.astype(jnp.float32) + shares).astype(jnp.bfloat16)

    if paired:
        final = lax.ppermute(mine, ("dp", "tensor"), turn)
    else:
        whole = lax.all_gather(mine, "tensor", axis=0, tiled=True)
        wide = lax.all_to_all(whole, "dp", split_axis=0, concat_axis=1, tiled=True)
        final = lax.dynamic_slice_in_dim(wide, my_group * local_width, local_width, 1)
    final = final.reshape(slots, seq_len, local_width)
    if sections == 2:
        half = seq_len // 2
        kept = lax.dynamic_slice_in_dim(final, my_section * half, half, 1)
        sent = lax.dynamic_slice_in_dim(final, (1 - my_section) * half, half, 1)
        came = swapped(sent, "pipe", 1)
        first = my_section == 0
        return jnp.concatenate([jnp.where(first, kept, came), jnp.where(first, came, kept)], axis=0)
    return lax.all_to_all(final, "pipe", split_axis=1, concat_axis=0, tiled=True)


def solution(mesh):
    placed = (
        P("dp", None, "tensor"),
        P(None, "pipe", "dp", "tensor"),
        P(None, "pipe", "dp", "tensor"),
        P(None, "pipe", "dp", "tensor"),
        P(None, "pipe", "tensor", "dp"),
        P(None, "pipe", None),
        P("dp"),
        P("dp"),
        P("dp", None),
        P("dp", None),
    )
    return jax.shard_map(
        per_device, mesh=mesh, in_specs=placed, out_specs=P("dp", "pipe", "tensor"), check_vma=False
    )
```

```python
from functools import partial

import jax
import jax.numpy as jnp
from jax import lax
from jax.experimental import pallas as pl
from jax.experimental.pallas import tpu as pltpu
from jax.sharding import PartitionSpec as P

HEAD_DIM = 128
LANES = 128
ROPE_THETA = 500000.0
NORM_EPSILON = 1e-05
VMEM_BYTES = 16 * 1024 * 1024


def unread(count, at, kernel):
    def wrapped(*refs):
        return kernel(*refs[:at], *refs[at + count :])

    return wrapped


def in_vmem(count):
    return [pl.BlockSpec(memory_space=pltpu.VMEM)] * count


def column_tiles(width, tile):
    return [(at, min(tile, width - at)) for at in range(0, width, tile)]


def qkv_kernel(n_in, n_out, part, *refs):
    if part is None:
        so_far, *shares = refs[: 1 + n_in]
    else:
        place, *blocks = refs[: 1 + n_in]
    gain, wq, wk, wv, stream = refs[1 + n_in : 6 + n_in]
    outs, (rows,) = refs[6 + n_in : 6 + n_in + n_out], refs[6 + n_in + n_out :]
    scale = gain[...]
    if part is None:
        sums = [share[...].astype(jnp.float32) for share in shares]
        while len(sums) > 1:
            sums = [sums[m] + sums[m + 1] if m + 1 < len(sums) else sums[m] for m in range(0, len(sums), 2)]
        stream[...] = (so_far[...].astype(jnp.float32) + sums[0]).astype(stream.dtype)
    else:
        size = stream.shape[0] // n_in
        for m, block in enumerate(blocks):
            at = pl.ds(pl.multiple_of(place[m] * size, size), size)
            stream[at, :] = block[part * size : (part + 1) * size]
    wide = stream[...].astype(jnp.float32)
    rows[...] = (wide * scale).astype(jnp.bfloat16)
    total = jnp.sum(wide * wide, axis=-1, keepdims=True)
    out_size = outs[0].shape[0]
    start = 0
    for weight in (wq, wk, wv):
        for at, width in column_tiles(weight.shape[1], 512):
            product = jnp.dot(rows[...], weight[:, at : at + width], preferred_element_type=jnp.float32)
            for m, out in enumerate(outs):
                piece = product[m * out_size : (m + 1) * out_size]
                out[:, start + at : start + at + width] = piece.astype(out.dtype)
        start += weight.shape[1]
    high = total.astype(jnp.bfloat16).astype(jnp.float32)
    lane = lax.broadcasted_iota(jnp.int32, (total.shape[0], LANES), 1)
    split = jnp.where(lane < LANES // 2, high, total - high)
    for m, out in enumerate(outs):
        out[:, start : start + LANES] = split[m * out_size : (m + 1) * out_size].astype(out.dtype)


def project_qkv(head, arrays, part, total, gain, wq, wk, wv, n_out, after):
    depth = wq.shape[0]
    columns = wq.shape[1] + wk.shape[1] + wv.shape[1] + LANES
    shapes = [jax.ShapeDtypeStruct((total, depth), jnp.bfloat16)] + [
        jax.ShapeDtypeStruct((total // n_out, columns), jnp.float32 if m == 0 and n_out > 1 else jnp.bfloat16)
        for m in range(n_out)
    ]
    first = in_vmem(1) if part is None else [pl.BlockSpec(memory_space=pltpu.SMEM)]
    stream, *sums = pl.pallas_call(
        unread(len(after), len(arrays) + 5, partial(qkv_kernel, len(arrays), n_out, part)),
        out_shape=shapes,
        in_specs=first + in_vmem(len(arrays) + 4 + len(after)),
        out_specs=in_vmem(1 + n_out),
        scratch_shapes=[pltpu.VMEM((total, depth), jnp.bfloat16)],
        compiler_params=pltpu.CompilerParams(vmem_limit_bytes=VMEM_BYTES),
        cost_estimate=pl.CostEstimate(flops=5499999999, bytes_accessed=1000, transcendentals=0),
        name="project_qkv",
    )(head, *arrays, gain, wq, wk, wv, *after)
    return stream, sums


def attention_kernel(n_in, n_before, q_heads, kv_heads, model_width, *refs):
    blocks, before, refs = refs[:n_in], refs[n_in : n_in + 2 * n_before], refs[n_in + 2 * n_before :]
    cosine, sine, mask, out, key_out, value_out = refs
    samples = cosine.shape[0]
    size = out.shape[0] // samples
    group = q_heads // kv_heads
    first = n_before * size

    def summed(rows, at, width):
        value = blocks[0][rows, at : at + width].astype(jnp.float32)
        for block in blocks[1:]:
            value = value + block[rows, at : at + width].astype(jnp.float32)
        return value

    k_at = q_heads * HEAD_DIM
    v_at = k_at + kv_heads * HEAD_DIM
    s_at = v_at + kv_heads * HEAD_DIM
    for s in range(samples):
        rows = slice(s * size, (s + 1) * size)
        parts = summed(rows, s_at, LANES)
        squares = parts[:, :1] + parts[:, LANES // 2 : LANES // 2 + 1]
        inverse = lax.rsqrt(squares * (1.0 / model_width) + NORM_EPSILON)
        cos, sin = cosine[s, first : first + size], sine[s, first : first + size]
        bias = mask[s, first : first + size, : first + size]

        def rotated(at):
            value = summed(rows, at, HEAD_DIM) * inverse
            turned = pltpu.roll(value, HEAD_DIM // 2, 1)
            return (value * cos + turned * sin).astype(jnp.bfloat16)

        bias_all = jnp.concatenate([bias] * group, axis=0)
        for kv in range(kv_heads):
            lanes = slice(kv * HEAD_DIM, (kv + 1) * HEAD_DIM)
            key = rotated(k_at + kv * HEAD_DIM)
            value = (summed(rows, v_at + kv * HEAD_DIM, HEAD_DIM) * inverse).astype(jnp.bfloat16)
            key_out[rows, lanes] = key
            value_out[rows, lanes] = value
            if n_before:
                key = jnp.concatenate([k[rows, lanes] for k in before[0::2]] + [key], axis=0)
                value = jnp.concatenate([v[rows, lanes] for v in before[1::2]] + [value], axis=0)
            query = jnp.concatenate([rotated((kv * group + g) * HEAD_DIM) for g in range(group)], axis=0)
            scores = lax.dot_general(query, key, (((1,), (1,)), ((), ())), preferred_element_type=jnp.float32)
            scores = scores * HEAD_DIM ** (-0.5) + bias_all
            top = jnp.max(scores, axis=-1, keepdims=True)
            weights = jnp.exp(scores - top)
            weights = weights / jnp.sum(weights, axis=-1, keepdims=True)
            mixed = jnp.dot(weights.astype(jnp.bfloat16), value, preferred_element_type=jnp.float32)
            for g in range(group):
                at = (kv * group + g) * HEAD_DIM
                out[rows, at : at + HEAD_DIM] = mixed[g * size : (g + 1) * size].astype(out.dtype)


def attend(blocks, before, cosine, sine, mask, q_heads, kv_heads, model_width, after):
    rows = blocks[0].shape[0]
    shapes = [(rows, heads * HEAD_DIM) for heads in (q_heads, kv_heads, kv_heads)]
    return pl.pallas_call(
        unread(
            len(after),
            len(blocks) + 2 * len(before) + 3,
            partial(attention_kernel, len(blocks), len(before), q_heads, kv_heads, model_width),
        ),
        out_shape=[jax.ShapeDtypeStruct(shape, jnp.bfloat16) for shape in shapes],
        in_specs=in_vmem(len(blocks) + 2 * len(before) + 3 + len(after)),
        out_specs=in_vmem(3),
        compiler_params=pltpu.CompilerParams(vmem_limit_bytes=VMEM_BYTES),
        cost_estimate=pl.CostEstimate(flops=5499999999, bytes_accessed=1000, transcendentals=0),
        name="attend",
    )(*blocks, *[array for pair in before for array in pair], cosine, sine, mask, *after)


def out_kernel(n_in, n_out, placed, *refs):
    place, refs = (refs[0], refs[1:]) if placed else (None, refs)
    blocks, weight = refs[:n_in], refs[n_in]
    outs, (rows,) = refs[n_in + 1 : n_in + 1 + n_out], refs[n_in + 1 + n_out :]
    size = blocks[0].shape[0]
    for m, block in enumerate(blocks):
        at = pl.multiple_of(place[m] * size, size) if placed else m * size
        rows[pl.ds(at, size), :] = block[...]
    out_size = outs[0].shape[0]
    for at, width in column_tiles(weight.shape[1], 512):
        product = jnp.dot(rows[...], weight[:, at : at + width], preferred_element_type=jnp.float32)
        for m, out in enumerate(outs):
            out[:, at : at + width] = product[m * out_size : (m + 1) * out_size].astype(out.dtype)


def project_out(blocks, place, weight, n_out, after):
    n_in = len(blocks)
    total = n_in * blocks[0].shape[0]
    depth, columns = weight.shape
    shapes = [
        jax.ShapeDtypeStruct((total // n_out, columns), jnp.float32 if m == 0 and n_out > 1 else jnp.bfloat16)
        for m in range(n_out)
    ]
    placed = place is not None
    return pl.pallas_call(
        unread(len(after), placed + n_in + 1, partial(out_kernel, n_in, n_out, placed)),
        out_shape=shapes,
        in_specs=[pl.BlockSpec(memory_space=pltpu.SMEM)] * placed + in_vmem(n_in + 1 + len(after)),
        out_specs=in_vmem(n_out),
        scratch_shapes=[pltpu.VMEM((total, depth), jnp.bfloat16)],
        compiler_params=pltpu.CompilerParams(vmem_limit_bytes=VMEM_BYTES),
        cost_estimate=pl.CostEstimate(flops=5499999999, bytes_accessed=1000, transcendentals=0),
        name="project_out",
    )(*([place] if placed else []), *blocks, weight, *after)


def pick_kernel(parts, slots, order, spot, tokens, out):
    size = out.shape[2]
    for s in range(slots):
        for h in range(parts):
            pltpu.sync_copy(tokens.at[order[0, spot[0] * slots + s], pl.ds(h * size, size)], out.at[h, s])


def pick_samples(tokens, order, spot, slots, parts):
    _, seq, width = tokens.shape
    smem = pl.BlockSpec(memory_space=pltpu.SMEM)
    return pl.pallas_call(
        partial(pick_kernel, parts, slots),
        out_shape=jax.ShapeDtypeStruct((parts, slots, seq // parts, width), tokens.dtype),
        in_specs=[smem, smem, pl.BlockSpec(memory_space=pl.ANY)],
        out_specs=pl.BlockSpec(memory_space=pltpu.VMEM),
        name="pick_samples",
    )(order, spot, tokens)


def layout_kernel(slots, spot, order, boundary, skip_offset, doc_lengths, frequency, _, angle, mask):
    seq, docs = mask.shape[1], doc_lengths.shape[1]
    for s in range(slots):
        sample = order[0, spot[0] * slots + s]
        place = lax.broadcasted_iota(jnp.int32, (seq, HEAD_DIM), 0)
        position = jnp.where(place < boundary[sample], place, place + skip_offset[sample])
        angle[s] = position.astype(jnp.float32) * frequency[...]
        row = lax.broadcasted_iota(jnp.int32, (seq, seq), 0)
        column = lax.broadcasted_iota(jnp.int32, (seq, seq), 1)
        row_doc, column_doc = jnp.zeros_like(row), jnp.zeros_like(row)
        end = jnp.int32(0)
        for k in range(docs):
            end = end + doc_lengths[sample, k]
            row_doc = row_doc + (row >= end).astype(jnp.int32)
            column_doc = column_doc + (column >= end).astype(jnp.int32)
        mask[s] = jnp.where((row_doc == column_doc) & (column <= row), 0.0, -jnp.inf)


def layout_of(order, boundary, skip_offset, doc_lengths, spot, slots, seq_len, after):
    half_dim = HEAD_DIM // 2
    exponent = jnp.arange(half_dim, dtype=jnp.float32) * (2.0 / HEAD_DIM)
    frequency = jnp.float32(ROPE_THETA) ** (-exponent)
    frequency = jnp.concatenate([frequency, frequency])[None]
    smem = pl.BlockSpec(memory_space=pltpu.SMEM)
    angle, mask = pl.pallas_call(
        partial(layout_kernel, slots),
        out_shape=[
            jax.ShapeDtypeStruct((slots, seq_len, HEAD_DIM), jnp.float32),
            jax.ShapeDtypeStruct((slots, seq_len, seq_len), jnp.float32),
        ],
        in_specs=[smem] * 5 + in_vmem(2),
        out_specs=in_vmem(2),
        name="layout",
    )(spot, order, boundary, skip_offset, doc_lengths, frequency, after)
    sign = jnp.where(jnp.arange(HEAD_DIM) < half_dim, -1.0, 1.0).astype(jnp.float32)
    return jnp.cos(angle), jnp.sin(angle) * sign, mask


def swapped(value, axis, by):
    return lax.ppermute(value, axis, [(i, i ^ by) for i in range(lax.axis_size(axis))])


def gather_blocks(block, axis, peers):
    return [block] + [swapped(block, axis, m) for m in range(1, peers)]


def trade_blocks(blocks, axis):
    return [blocks[0]] + [swapped(blocks[m], axis, m) for m in range(1, len(blocks))]


def total_of(blocks):
    value = blocks[0].astype(jnp.float32)
    for block in blocks[1:]:
        value = value + block.astype(jnp.float32)
    return value


def per_device(
    tokens,
    w_query,
    w_key,
    w_value,
    w_out,
    norm_gain,
    boundary,
    skip_offset,
    doc_lengths,
    batch_order,
):
    replicas, sections, groups = lax.axis_size("dp"), lax.axis_size("pipe"), lax.axis_size("tensor")
    my_replica, my_section, my_group = lax.axis_index("dp"), lax.axis_index("pipe"), lax.axis_index("tensor")
    micro_count, seq_len, local_width = tokens.shape
    model_width = local_width * groups
    slots = micro_count // sections
    rows = slots * seq_len
    depth = w_query.shape[2]
    q_heads = w_query.shape[3] // HEAD_DIM
    kv_heads = w_key.shape[3] // HEAD_DIM
    paired = replicas == groups and replicas & (replicas - 1) == 0

    spot = jnp.reshape(my_section, (1,)).astype(jnp.int32)
    parts = 2 if paired else 1
    part_len = seq_len // parts
    stream = pick_samples(tokens, batch_order, spot, slots, parts).reshape(rows, local_width)

    gain_rows = lax.dynamic_slice_in_dim(norm_gain, my_replica * depth, depth, 2)
    held = (w_query, w_key, w_value, w_out)
    if sections == 2:
        gain_traded = swapped(gain_rows, "pipe", 1)
        gain_traded, held = lax.optimization_barrier((gain_traded, held))
        held = (gain_rows, *held)
        traded = [gain_traded] + [swapped(w, "pipe", 1) for w in held[1:]]

        def layer_weights(index, section):
            return [
                jnp.where(my_section == section, mine[index, 0], theirs[index, 0])
                for mine, theirs in zip(held, traded)
            ]
    else:
        gathered = [lax.all_gather(w, "pipe", axis=1, tiled=True) for w in (gain_rows, *held)]

        def layer_weights(index, section):
            return [w[index, section] for w in gathered]

    turn = [(i * groups + j, j * groups + i) for i in range(replicas) for j in range(groups)]
    if paired:
        place = lax.bitwise_xor(jnp.arange(groups, dtype=jnp.int32), lax.bitwise_xor(my_replica, my_group))
        blocks = gather_blocks(lax.ppermute(stream, ("dp", "tensor"), turn), "tensor", groups)
    else:
        place = jnp.zeros((1,), jnp.int32)
        wide = lax.all_gather(stream, "tensor", axis=1, tiled=True)
        blocks = [lax.all_to_all(wide, "dp", split_axis=1, concat_axis=0, tiled=True)]
    part_rows = slots * part_len
    total = replicas * part_rows

    layout, latest = None, []
    layers = [(0, s) for s in range(sections)] + [(1, s) for s in reversed(range(sections))]
    streams, shares = [None] * parts, [None] * parts
    for number, (index, section) in enumerate(layers):
        gain, wq, wk, wv, wo = layer_weights(index, section)
        last = number + 1 == len(layers)
        before, sums, mixed = [], [None] * parts, [None] * parts
        for h in range(parts):
            head, arrays, part = (streams[h], shares[h], None) if number else (place, blocks, h)
            streams[h], sums[h] = project_qkv(
                head, arrays, part, total, gain[None], wq, wk, wv, replicas if paired else 1, latest
            )
            latest = [streams[h]]
            if layout is None:
                layout = layout_of(
                    batch_order, boundary, skip_offset, doc_lengths, spot, slots, seq_len, sums[0][0]
                )
            if paired:
                sums[h] = trade_blocks(sums[h], "dp")
            else:
                pieces = sums[h][0].reshape(replicas, part_rows, sums[h][0].shape[1])
                pieces = lax.all_to_all(pieces, "dp", split_axis=0, concat_axis=0)
                sums[h] = [jnp.sum(pieces.astype(jnp.float32), axis=0)]
        for h in range(parts):
            mixed[h], keys, values = attend(
                sums[h], before, *layout, q_heads, kv_heads, model_width, latest
            )
            latest = [keys]
            before.append((keys, values))
            if paired:
                mixed[h] = gather_blocks(mixed[h], "dp", replicas)
            else:
                mixed[h] = [lax.all_gather(mixed[h], "dp", axis=0, tiled=True)]
        for h in range(parts):
            ends = project_out(
                mixed[h], place if paired and last else None, wo, groups if paired and last else 1, latest
            )
            latest = ends[:1]
            if not paired:
                shares[h] = [lax.psum(ends[0].astype(jnp.float32), "tensor")]
            elif last:
                shares[h] = trade_blocks(ends, "tensor")
            else:
                shares[h] = gather_blocks(ends[0], "tensor", groups)

    final = []
    for stream, share in zip(streams, shares):
        share = total_of(share)
        if paired:
            stream = lax.dynamic_slice_in_dim(stream, place[0] * part_rows, part_rows, 0)
            stream = (stream.astype(jnp.float32) + share).astype(jnp.bfloat16)
            stream = lax.ppermute(stream, ("dp", "tensor"), turn)
        else:
            stream = (stream.astype(jnp.float32) + share).astype(jnp.bfloat16)
            stream = lax.all_to_all(stream, "dp", split_axis=0, concat_axis=1, tiled=True)
            stream = lax.dynamic_slice_in_dim(stream, my_group * local_width, local_width, 1)
        final.append(stream.reshape(slots, part_len, local_width))
    if parts == sections == 2:
        first = my_section == 0
        came = swapped(jnp.where(first, final[1], final[0]), "pipe", 1)
        kept = jnp.where(first, final[0], final[1])
        return jnp.concatenate([jnp.where(first, kept, came), jnp.where(first, came, kept)], axis=0)
    final = jnp.concatenate(final, axis=1)
    return lax.all_to_all(final, "pipe", split_axis=1, concat_axis=0, tiled=True)


def solution(mesh):
    placed = (
        P("dp", None, "tensor"),
        P(None, "pipe", "dp", "tensor"),
        P(None, "pipe", "dp", "tensor"),
        P(None, "pipe", "dp", "tensor"),
        P(None, "pipe", "tensor", "dp"),
        P(None, "pipe", None),
        P("dp"),
        P("dp"),
        P("dp", None),
        P("dp", None),
    )
    return jax.shard_map(
        per_device, mesh=mesh, in_specs=placed, out_specs=P("dp", "pipe", "tensor"), check_vma=False
    )
```

```python
from functools import partial

import jax
import jax.numpy as jnp
from jax import lax
from jax.experimental import pallas as pl
from jax.experimental.pallas import tpu as pltpu
from jax.sharding import PartitionSpec as P

HEAD_DIM = 128
LANES = 128
ROPE_THETA = 500000.0
NORM_EPSILON = 1e-05
VMEM_BYTES = 8 * 1024 * 1024
STEP_FLOPS = 5_500_000_000


def unread(count, at, kernel):
    def wrapped(*refs):
        return kernel(*refs[:at], *refs[at + count :])

    return wrapped


def in_vmem(count):
    return [pl.BlockSpec(memory_space=pltpu.VMEM)] * count


def column_tiles(width, tile):
    return [(at, min(tile, width - at)) for at in range(0, width, tile)]


def qkv_kernel(n_in, n_out, part, *refs):
    if part is None:
        so_far, *shares = refs[: 1 + n_in]
    else:
        place, *blocks = refs[: 1 + n_in]
    gain, wq, wk, wv, stream = refs[1 + n_in : 6 + n_in]
    outs, (rows,) = refs[6 + n_in : 6 + n_in + n_out], refs[6 + n_in + n_out :]
    scale = gain[...]
    if part is None:
        sums = [share[...].astype(jnp.float32) for share in shares]
        while len(sums) > 1:
            sums = [sums[m] + sums[m + 1] if m + 1 < len(sums) else sums[m] for m in range(0, len(sums), 2)]
        stream[...] = (so_far[...].astype(jnp.float32) + sums[0]).astype(stream.dtype)
    else:
        size = stream.shape[0] // n_in
        for m, block in enumerate(blocks):
            at = pl.ds(pl.multiple_of(place[m] * size, size), size)
            stream[at, :] = block[part * size : (part + 1) * size]
    wide = stream[...].astype(jnp.float32)
    rows[...] = (wide * scale).astype(jnp.bfloat16)
    total = jnp.sum(wide * wide, axis=-1, keepdims=True)
    out_size = outs[0].shape[0]
    start = 0
    for weight in (wq, wk, wv):
        for at, width in column_tiles(weight.shape[1], 512):
            product = jnp.dot(rows[...], weight[:, at : at + width], preferred_element_type=jnp.float32)
            for m, out in enumerate(outs):
                piece = product[m * out_size : (m + 1) * out_size]
                out[:, start + at : start + at + width] = piece.astype(out.dtype)
        start += weight.shape[1]
    high = total.astype(jnp.bfloat16).astype(jnp.float32)
    lane = lax.broadcasted_iota(jnp.int32, (total.shape[0], LANES), 1)
    split = jnp.where(lane < LANES // 2, high, total - high)
    for m, out in enumerate(outs):
        out[:, start : start + LANES] = split[m * out_size : (m + 1) * out_size].astype(out.dtype)


def project_qkv(head, arrays, part, total, gain, wq, wk, wv, n_out, after):
    depth = wq.shape[0]
    columns = wq.shape[1] + wk.shape[1] + wv.shape[1] + LANES
    shapes = [jax.ShapeDtypeStruct((total, depth), jnp.bfloat16)] + [
        jax.ShapeDtypeStruct((total // n_out, columns), jnp.float32 if m == 0 and n_out > 1 else jnp.bfloat16)
        for m in range(n_out)
    ]
    first = in_vmem(1) if part is None else [pl.BlockSpec(memory_space=pltpu.SMEM)]
    stream, *sums = pl.pallas_call(
        unread(len(after), len(arrays) + 5, partial(qkv_kernel, len(arrays), n_out, part)),
        out_shape=shapes,
        in_specs=first + in_vmem(len(arrays) + 4 + len(after)),
        out_specs=in_vmem(1 + n_out),
        scratch_shapes=[pltpu.VMEM((total, depth), jnp.bfloat16)],
        compiler_params=pltpu.CompilerParams(vmem_limit_bytes=VMEM_BYTES),
        cost_estimate=pl.CostEstimate(flops=STEP_FLOPS, bytes_accessed=1000, transcendentals=0),
        name="project_qkv",
    )(head, *arrays, gain, wq, wk, wv, *after)
    return stream, sums


def attention_kernel(n_in, n_before, q_heads, kv_heads, model_width, *refs):
    blocks, before, refs = refs[:n_in], refs[n_in : n_in + 2 * n_before], refs[n_in + 2 * n_before :]
    cosine, sine, mask, out, key_out, value_out = refs
    samples = cosine.shape[0]
    size = out.shape[0] // samples
    group = q_heads // kv_heads
    first = n_before * size

    def summed(rows, at, width):
        value = blocks[0][rows, at : at + width].astype(jnp.float32)
        for block in blocks[1:]:
            value = value + block[rows, at : at + width].astype(jnp.float32)
        return value

    k_at = q_heads * HEAD_DIM
    v_at = k_at + kv_heads * HEAD_DIM
    s_at = v_at + kv_heads * HEAD_DIM
    for s in range(samples):
        rows = slice(s * size, (s + 1) * size)
        parts = summed(rows, s_at, LANES)
        squares = parts[:, :1] + parts[:, LANES // 2 : LANES // 2 + 1]
        inverse = lax.rsqrt(squares * (1.0 / model_width) + NORM_EPSILON)
        cos, sin = cosine[s, first : first + size], sine[s, first : first + size]
        bias = mask[s, first : first + size, : first + size]

        def rotated(at):
            value = summed(rows, at, HEAD_DIM) * inverse
            turned = pltpu.roll(value, HEAD_DIM // 2, 1)
            return (value * cos + turned * sin).astype(jnp.bfloat16)

        bias_all = jnp.concatenate([bias] * group, axis=0)
        for kv in range(kv_heads):
            lanes = slice(kv * HEAD_DIM, (kv + 1) * HEAD_DIM)
            key = rotated(k_at + kv * HEAD_DIM)
            value = (summed(rows, v_at + kv * HEAD_DIM, HEAD_DIM) * inverse).astype(jnp.bfloat16)
            key_out[rows, lanes] = key
            value_out[rows, lanes] = value
            if n_before:
                key = jnp.concatenate([k[rows, lanes] for k in before[0::2]] + [key], axis=0)
                value = jnp.concatenate([v[rows, lanes] for v in before[1::2]] + [value], axis=0)
            query = jnp.concatenate([rotated((kv * group + g) * HEAD_DIM) for g in range(group)], axis=0)
            scores = lax.dot_general(query, key, (((1,), (1,)), ((), ())), preferred_element_type=jnp.float32)
            scores = scores * HEAD_DIM ** (-0.5) + bias_all
            top = jnp.max(scores, axis=-1, keepdims=True)
            weights = jnp.exp(scores - top)
            weights = weights / jnp.sum(weights, axis=-1, keepdims=True)
            mixed = jnp.dot(weights.astype(jnp.bfloat16), value, preferred_element_type=jnp.float32)
            for g in range(group):
                at = (kv * group + g) * HEAD_DIM
                out[rows, at : at + HEAD_DIM] = mixed[g * size : (g + 1) * size].astype(out.dtype)


def attend(blocks, before, cosine, sine, mask, q_heads, kv_heads, model_width, after):
    rows = blocks[0].shape[0]
    shapes = [(rows, heads * HEAD_DIM) for heads in (q_heads, kv_heads, kv_heads)]
    return pl.pallas_call(
        unread(
            len(after),
            len(blocks) + 2 * len(before) + 3,
            partial(attention_kernel, len(blocks), len(before), q_heads, kv_heads, model_width),
        ),
        out_shape=[jax.ShapeDtypeStruct(shape, jnp.bfloat16) for shape in shapes],
        in_specs=in_vmem(len(blocks) + 2 * len(before) + 3 + len(after)),
        out_specs=in_vmem(3),
        compiler_params=pltpu.CompilerParams(vmem_limit_bytes=VMEM_BYTES),
        cost_estimate=pl.CostEstimate(flops=STEP_FLOPS, bytes_accessed=1000, transcendentals=0),
        name="attend",
    )(*blocks, *[array for pair in before for array in pair], cosine, sine, mask, *after)


def out_kernel(n_in, n_out, placed, *refs):
    place, refs = (refs[0], refs[1:]) if placed else (None, refs)
    blocks, weight = refs[:n_in], refs[n_in]
    outs, (rows,) = refs[n_in + 1 : n_in + 1 + n_out], refs[n_in + 1 + n_out :]
    size = blocks[0].shape[0]
    for m, block in enumerate(blocks):
        at = pl.multiple_of(place[m] * size, size) if placed else m * size
        rows[pl.ds(at, size), :] = block[...]
    out_size = outs[0].shape[0]
    for at, width in column_tiles(weight.shape[1], 512):
        product = jnp.dot(rows[...], weight[:, at : at + width], preferred_element_type=jnp.float32)
        for m, out in enumerate(outs):
            out[:, at : at + width] = product[m * out_size : (m + 1) * out_size].astype(out.dtype)


def project_out(blocks, place, weight, n_out, after):
    n_in = len(blocks)
    total = n_in * blocks[0].shape[0]
    depth, columns = weight.shape
    shapes = [
        jax.ShapeDtypeStruct((total // n_out, columns), jnp.float32 if m == 0 and n_out > 1 else jnp.bfloat16)
        for m in range(n_out)
    ]
    placed = place is not None
    return pl.pallas_call(
        unread(len(after), placed + n_in + 1, partial(out_kernel, n_in, n_out, placed)),
        out_shape=shapes,
        in_specs=[pl.BlockSpec(memory_space=pltpu.SMEM)] * placed + in_vmem(n_in + 1 + len(after)),
        out_specs=in_vmem(n_out),
        scratch_shapes=[pltpu.VMEM((total, depth), jnp.bfloat16)],
        compiler_params=pltpu.CompilerParams(vmem_limit_bytes=VMEM_BYTES),
        cost_estimate=pl.CostEstimate(flops=STEP_FLOPS, bytes_accessed=1000, transcendentals=0),
        name="project_out",
    )(*([place] if placed else []), *blocks, weight, *after)


def pick_kernel(parts, slots, order, spot, tokens, out):
    size = out.shape[2]
    for s in range(slots):
        for h in range(parts):
            pltpu.sync_copy(tokens.at[order[0, spot[0] * slots + s], pl.ds(h * size, size)], out.at[h, s])


def pick_samples(tokens, order, spot, slots, parts):
    _, seq, width = tokens.shape
    smem = pl.BlockSpec(memory_space=pltpu.SMEM)
    return pl.pallas_call(
        partial(pick_kernel, parts, slots),
        out_shape=jax.ShapeDtypeStruct((parts, slots, seq // parts, width), tokens.dtype),
        in_specs=[smem, smem, pl.BlockSpec(memory_space=pl.ANY)],
        out_specs=pl.BlockSpec(memory_space=pltpu.VMEM),
        compiler_params=pltpu.CompilerParams(vmem_limit_bytes=VMEM_BYTES),
        name="pick_samples",
    )(order, spot, tokens)


def layout_kernel(slots, spot, order, boundary, skip_offset, doc_lengths, frequency, _, angle, mask):
    seq, docs = mask.shape[1], doc_lengths.shape[1]
    for s in range(slots):
        sample = order[0, spot[0] * slots + s]
        place = lax.broadcasted_iota(jnp.int32, (seq, HEAD_DIM), 0)
        position = jnp.where(place < boundary[sample], place, place + skip_offset[sample])
        angle[s] = position.astype(jnp.float32) * frequency[...]
        row = lax.broadcasted_iota(jnp.int32, (seq, seq), 0)
        column = lax.broadcasted_iota(jnp.int32, (seq, seq), 1)
        row_doc, column_doc = jnp.zeros_like(row), jnp.zeros_like(row)
        end = jnp.int32(0)
        for k in range(docs):
            end = end + doc_lengths[sample, k]
            row_doc = row_doc + (row >= end).astype(jnp.int32)
            column_doc = column_doc + (column >= end).astype(jnp.int32)
        mask[s] = jnp.where((row_doc == column_doc) & (column <= row), 0.0, -jnp.inf)


def layout_of(order, boundary, skip_offset, doc_lengths, spot, slots, seq_len, after):
    half_dim = HEAD_DIM // 2
    exponent = jnp.arange(half_dim, dtype=jnp.float32) * (2.0 / HEAD_DIM)
    frequency = jnp.float32(ROPE_THETA) ** (-exponent)
    frequency = jnp.concatenate([frequency, frequency])[None]
    smem = pl.BlockSpec(memory_space=pltpu.SMEM)
    angle, mask = pl.pallas_call(
        partial(layout_kernel, slots),
        out_shape=[
            jax.ShapeDtypeStruct((slots, seq_len, HEAD_DIM), jnp.float32),
            jax.ShapeDtypeStruct((slots, seq_len, seq_len), jnp.float32),
        ],
        in_specs=[smem] * 5 + in_vmem(2),
        out_specs=in_vmem(2),
        compiler_params=pltpu.CompilerParams(vmem_limit_bytes=VMEM_BYTES),
        name="layout",
    )(spot, order, boundary, skip_offset, doc_lengths, frequency, after)
    sign = jnp.where(jnp.arange(HEAD_DIM) < half_dim, -1.0, 1.0).astype(jnp.float32)
    return jnp.cos(angle), jnp.sin(angle) * sign, mask


def swapped(value, axis, by):
    return lax.ppermute(value, axis, [(i, i ^ by) for i in range(lax.axis_size(axis))])


def gather_blocks(block, axis, peers):
    return [block] + [swapped(block, axis, m) for m in range(1, peers)]


def trade_blocks(blocks, axis):
    return [blocks[0]] + [swapped(blocks[m], axis, m) for m in range(1, len(blocks))]


def total_of(blocks):
    value = blocks[0].astype(jnp.float32)
    for block in blocks[1:]:
        value = value + block.astype(jnp.float32)
    return value


def steps_of(parts, layers):
    if parts == 1:
        return [(step, 0, number) for number in range(layers) for step in range(3)]
    steps = [(0, 0, 0), (1, 0, 0), (0, 1, 0), (2, 0, 0), (1, 1, 0)]
    for number in range(1, layers):
        steps += [(0, 0, number), (2, 1, number - 1), (1, 0, number), (0, 1, number), (2, 0, number), (1, 1, number)]
    return steps + [(2, 1, layers - 1)]


def per_device(
    tokens,
    w_query,
    w_key,
    w_value,
    w_out,
    norm_gain,
    boundary,
    skip_offset,
    doc_lengths,
    batch_order,
):
    replicas, sections, groups = lax.axis_size("dp"), lax.axis_size("pipe"), lax.axis_size("tensor")
    my_replica, my_section, my_group = lax.axis_index("dp"), lax.axis_index("pipe"), lax.axis_index("tensor")
    micro_count, seq_len, local_width = tokens.shape
    model_width = local_width * groups
    slots = micro_count // sections
    rows = slots * seq_len
    depth = w_query.shape[2]
    q_heads = w_query.shape[3] // HEAD_DIM
    kv_heads = w_key.shape[3] // HEAD_DIM
    paired = replicas == groups and replicas & (replicas - 1) == 0

    spot = jnp.reshape(my_section, (1,)).astype(jnp.int32)
    parts = 2 if paired else 1
    part_len = seq_len // parts
    stream = pick_samples(tokens, batch_order, spot, slots, parts).reshape(rows, local_width)

    gain_rows = lax.dynamic_slice_in_dim(norm_gain, my_replica * depth, depth, 2)
    held = (w_query, w_key, w_value, w_out)
    if sections == 2:
        gain_traded = swapped(gain_rows, "pipe", 1)
        gain_traded, held = lax.optimization_barrier((gain_traded, held))
        held = (gain_rows, *held)
        traded = [gain_traded] + [swapped(w, "pipe", 1) for w in held[1:]]

        def layer_weights(index, section):
            return [
                jnp.where(my_section == section, mine[index, 0], theirs[index, 0])
                for mine, theirs in zip(held, traded)
            ]
    else:
        gathered = [lax.all_gather(w, "pipe", axis=1, tiled=True) for w in (gain_rows, *held)]

        def layer_weights(index, section):
            return [w[index, section] for w in gathered]

    turn = [(i * groups + j, j * groups + i) for i in range(replicas) for j in range(groups)]
    if paired:
        place = lax.bitwise_xor(jnp.arange(groups, dtype=jnp.int32), lax.bitwise_xor(my_replica, my_group))
        blocks = gather_blocks(lax.ppermute(stream, ("dp", "tensor"), turn), "tensor", groups)
    else:
        place = jnp.zeros((1,), jnp.int32)
        wide = lax.all_gather(stream, "tensor", axis=1, tiled=True)
        blocks = [lax.all_to_all(wide, "dp", split_axis=1, concat_axis=0, tiled=True)]
    part_rows = slots * part_len
    total = replicas * part_rows

    layers = [(0, s) for s in range(sections)] + [(1, s) for s in reversed(range(sections))]
    weights = [layer_weights(*layer) for layer in layers]
    streams, sums, mixed, shares = ([None] * parts for _ in range(4))
    before = [[] for _ in layers]
    layout, latest = None, []

    def share_out(h, number):
        nonlocal layout, latest
        gain, wq, wk, wv, _ = weights[number]
        head, arrays, part = (streams[h], shares[h], None) if number else (place, blocks, h)
        streams[h], ends = project_qkv(
            head, arrays, part, total, gain[None], wq, wk, wv, replicas if paired else 1, latest
        )
        latest = [streams[h]]
        if layout is None:
            layout = layout_of(batch_order, boundary, skip_offset, doc_lengths, spot, slots, seq_len, ends[0])
        if paired:
            sums[h] = trade_blocks(ends, "dp")
        else:
            pieces = ends[0].reshape(replicas, part_rows, ends[0].shape[1])
            pieces = lax.all_to_all(pieces, "dp", split_axis=0, concat_axis=0)
            sums[h] = [jnp.sum(pieces.astype(jnp.float32), axis=0)]

    def mix(h, number):
        nonlocal latest
        rows_out, keys, values = attend(
            sums[h], before[number], *layout, q_heads, kv_heads, model_width, latest
        )
        latest = [keys]
        before[number].append((keys, values))
        if paired:
            mixed[h] = gather_blocks(rows_out, "dp", replicas)
        else:
            mixed[h] = [lax.all_gather(rows_out, "dp", axis=0, tiled=True)]

    def bring_in(h, number):
        nonlocal latest
        last = number + 1 == len(layers)
        ends = project_out(
            mixed[h],
            place if paired and last else None,
            weights[number][4],
            groups if paired and last else 1,
            latest,
        )
        latest = ends[:1]
        if not paired:
            shares[h] = [lax.psum(ends[0].astype(jnp.float32), "tensor")]
        elif last:
            shares[h] = trade_blocks(ends, "tensor")
        else:
            shares[h] = gather_blocks(ends[0], "tensor", groups)

    for step, h, number in steps_of(parts, len(layers)):
        (share_out, mix, bring_in)[step](h, number)

    final = []
    for stream, share in zip(streams, shares):
        share = total_of(share)
        if paired:
            stream = lax.dynamic_slice_in_dim(stream, place[0] * part_rows, part_rows, 0)
            stream = (stream.astype(jnp.float32) + share).astype(jnp.bfloat16)
            stream = lax.ppermute(stream, ("dp", "tensor"), turn)
        else:
            stream = (stream.astype(jnp.float32) + share).astype(jnp.bfloat16)
            stream = lax.all_to_all(stream, "dp", split_axis=0, concat_axis=1, tiled=True)
            stream = lax.dynamic_slice_in_dim(stream, my_group * local_width, local_width, 1)
        final.append(stream.reshape(slots, part_len, local_width))
    if parts == sections == 2:
        first = my_section == 0
        came = swapped(jnp.where(first, final[1], final[0]), "pipe", 1)
        kept = jnp.where(first, final[0], final[1])
        return jnp.concatenate([jnp.where(first, kept, came), jnp.where(first, came, kept)], axis=0)
    final = jnp.concatenate(final, axis=1)
    return lax.all_to_all(final, "pipe", split_axis=1, concat_axis=0, tiled=True)


def solution(mesh):
    placed = (
        P("dp", None, "tensor"),
        P(None, "pipe", "dp", "tensor"),
        P(None, "pipe", "dp", "tensor"),
        P(None, "pipe", "dp", "tensor"),
        P(None, "pipe", "tensor", "dp"),
        P(None, "pipe", None),
        P("dp"),
        P("dp"),
        P("dp", None),
        P("dp", None),
    )
    return jax.shard_map(
        per_device, mesh=mesh, in_specs=placed, out_specs=P("dp", "pipe", "tensor"), check_vma=False
    )
```

```python
from functools import partial

import jax
import jax.numpy as jnp
from jax import lax
from jax.experimental import pallas as pl
from jax.experimental.pallas import tpu as pltpu
from jax.sharding import PartitionSpec as P

HEAD_DIM = 128
LANES = 128
ROPE_THETA = 500000.0
NORM_EPSILON = 1e-05
VMEM_BYTES = 8 * 1024 * 1024
STEP_FLOPS = 5_500_000_000


def unread(count, at, kernel):
    def wrapped(*refs):
        return kernel(*refs[:at], *refs[at + count :])

    return wrapped


def in_vmem(count):
    return [pl.BlockSpec(memory_space=pltpu.VMEM)] * count


def column_tiles(width, tile):
    return [(at, min(tile, width - at)) for at in range(0, width, tile)]


def qkv_kernel(n_in, n_out, part, *refs):
    if part is None:
        so_far, *shares = refs[: 1 + n_in]
    else:
        place, *blocks = refs[: 1 + n_in]
    gain, wq, wk, wv, stream = refs[1 + n_in : 6 + n_in]
    outs, (rows,) = refs[6 + n_in : 6 + n_in + n_out], refs[6 + n_in + n_out :]
    scale = gain[...]
    if part is None:
        sums = [share[...].astype(jnp.float32) for share in shares]
        while len(sums) > 1:
            sums = [sums[m] + sums[m + 1] if m + 1 < len(sums) else sums[m] for m in range(0, len(sums), 2)]
        stream[...] = (so_far[...].astype(jnp.float32) + sums[0]).astype(stream.dtype)
    else:
        size = stream.shape[0] // n_in
        for m, block in enumerate(blocks):
            at = pl.ds(pl.multiple_of(place[m] * size, size), size)
            stream[at, :] = block[part * size : (part + 1) * size]
    wide = stream[...].astype(jnp.float32)
    rows[...] = (wide * scale).astype(jnp.bfloat16)
    total = jnp.sum(wide * wide, axis=-1, keepdims=True)
    out_size = outs[0].shape[0]
    start = 0
    for weight in (wq, wk, wv):
        for at, width in column_tiles(weight.shape[1], 512):
            product = jnp.dot(rows[...], weight[:, at : at + width], preferred_element_type=jnp.float32)
            for m, out in enumerate(outs):
                piece = product[m * out_size : (m + 1) * out_size]
                out[:, start + at : start + at + width] = piece.astype(out.dtype)
        start += weight.shape[1]
    high = total.astype(jnp.bfloat16).astype(jnp.float32)
    lane = lax.broadcasted_iota(jnp.int32, (total.shape[0], LANES), 1)
    split = jnp.where(lane < LANES // 2, high, total - high)
    for m, out in enumerate(outs):
        out[:, start : start + LANES] = split[m * out_size : (m + 1) * out_size].astype(out.dtype)


def project_qkv(head, arrays, part, total, gain, wq, wk, wv, n_out, after):
    depth = wq.shape[0]
    columns = wq.shape[1] + wk.shape[1] + wv.shape[1] + LANES
    shapes = [jax.ShapeDtypeStruct((total, depth), jnp.bfloat16)] + [
        jax.ShapeDtypeStruct((total // n_out, columns), jnp.float32 if m == 0 and n_out > 1 else jnp.bfloat16)
        for m in range(n_out)
    ]
    first = in_vmem(1) if part is None else [pl.BlockSpec(memory_space=pltpu.SMEM)]
    stream, *sums = pl.pallas_call(
        unread(len(after), len(arrays) + 5, partial(qkv_kernel, len(arrays), n_out, part)),
        out_shape=shapes,
        in_specs=first + in_vmem(len(arrays) + 4 + len(after)),
        out_specs=in_vmem(1 + n_out),
        scratch_shapes=[pltpu.VMEM((total, depth), jnp.bfloat16)],
        compiler_params=pltpu.CompilerParams(vmem_limit_bytes=VMEM_BYTES),
        cost_estimate=pl.CostEstimate(flops=STEP_FLOPS, bytes_accessed=1000, transcendentals=0),
        name="project_qkv",
    )(head, *arrays, gain, wq, wk, wv, *after)
    return stream, sums


def attention_kernel(n_in, n_before, q_heads, kv_heads, model_width, *refs):
    blocks, before, refs = refs[:n_in], refs[n_in : n_in + 2 * n_before], refs[n_in + 2 * n_before :]
    cosine, sine, mask, out, key_out, value_out = refs
    samples = cosine.shape[0]
    size = out.shape[0] // samples
    group = q_heads // kv_heads
    first = n_before * size

    def summed(rows, at, width):
        value = blocks[0][rows, at : at + width].astype(jnp.float32)
        for block in blocks[1:]:
            value = value + block[rows, at : at + width].astype(jnp.float32)
        return value

    k_at = q_heads * HEAD_DIM
    v_at = k_at + kv_heads * HEAD_DIM
    s_at = v_at + kv_heads * HEAD_DIM
    for s in range(samples):
        rows = slice(s * size, (s + 1) * size)
        parts = summed(rows, s_at, LANES)
        squares = parts[:, :1] + parts[:, LANES // 2 : LANES // 2 + 1]
        inverse = lax.rsqrt(squares * (1.0 / model_width) + NORM_EPSILON)
        cos, sin = cosine[s, first : first + size], sine[s, first : first + size]
        bias = mask[s, first : first + size, : first + size]

        def rotated(at):
            value = summed(rows, at, HEAD_DIM) * inverse
            turned = pltpu.roll(value, HEAD_DIM // 2, 1)
            return (value * cos + turned * sin).astype(jnp.bfloat16)

        bias_all = jnp.concatenate([bias] * group, axis=0)
        for kv in range(kv_heads):
            lanes = slice(kv * HEAD_DIM, (kv + 1) * HEAD_DIM)
            key = rotated(k_at + kv * HEAD_DIM)
            value = (summed(rows, v_at + kv * HEAD_DIM, HEAD_DIM) * inverse).astype(jnp.bfloat16)
            key_out[rows, lanes] = key
            value_out[rows, lanes] = value
            if n_before:
                key = jnp.concatenate([k[rows, lanes] for k in before[0::2]] + [key], axis=0)
                value = jnp.concatenate([v[rows, lanes] for v in before[1::2]] + [value], axis=0)
            query = jnp.concatenate([rotated((kv * group + g) * HEAD_DIM) for g in range(group)], axis=0)
            scores = lax.dot_general(query, key, (((1,), (1,)), ((), ())), preferred_element_type=jnp.float32)
            scores = scores * HEAD_DIM ** (-0.5) + bias_all
            top = jnp.max(scores, axis=-1, keepdims=True)
            weights = jnp.exp(scores - top)
            weights = weights / jnp.sum(weights, axis=-1, keepdims=True)
            mixed = jnp.dot(weights.astype(jnp.bfloat16), value, preferred_element_type=jnp.float32)
            for g in range(group):
                at = (kv * group + g) * HEAD_DIM
                out[rows, at : at + HEAD_DIM] = mixed[g * size : (g + 1) * size].astype(out.dtype)


def attend(blocks, before, cosine, sine, mask, q_heads, kv_heads, model_width, after):
    rows = blocks[0].shape[0]
    shapes = [(rows, heads * HEAD_DIM) for heads in (q_heads, kv_heads, kv_heads)]
    return pl.pallas_call(
        unread(
            len(after),
            len(blocks) + 2 * len(before) + 3,
            partial(attention_kernel, len(blocks), len(before), q_heads, kv_heads, model_width),
        ),
        out_shape=[jax.ShapeDtypeStruct(shape, jnp.bfloat16) for shape in shapes],
        in_specs=in_vmem(len(blocks) + 2 * len(before) + 3 + len(after)),
        out_specs=in_vmem(3),
        compiler_params=pltpu.CompilerParams(vmem_limit_bytes=VMEM_BYTES),
        cost_estimate=pl.CostEstimate(flops=STEP_FLOPS, bytes_accessed=1000, transcendentals=0),
        name="attend",
    )(*blocks, *[array for pair in before for array in pair], cosine, sine, mask, *after)


def out_kernel(n_in, n_out, placed, *refs):
    place, refs = (refs[0], refs[1:]) if placed else (None, refs)
    blocks, weight = refs[:n_in], refs[n_in]
    outs, (rows,) = refs[n_in + 1 : n_in + 1 + n_out], refs[n_in + 1 + n_out :]
    size = blocks[0].shape[0]
    for m, block in enumerate(blocks):
        at = pl.multiple_of(place[m] * size, size) if placed else m * size
        rows[pl.ds(at, size), :] = block[...]
    out_size = outs[0].shape[0]
    for at, width in column_tiles(weight.shape[1], 512):
        product = jnp.dot(rows[...], weight[:, at : at + width], preferred_element_type=jnp.float32)
        for m, out in enumerate(outs):
            out[:, at : at + width] = product[m * out_size : (m + 1) * out_size].astype(out.dtype)


def project_out(blocks, place, weight, n_out, after):
    n_in = len(blocks)
    total = n_in * blocks[0].shape[0]
    depth, columns = weight.shape
    shapes = [
        jax.ShapeDtypeStruct((total // n_out, columns), jnp.float32 if m == 0 and n_out > 1 else jnp.bfloat16)
        for m in range(n_out)
    ]
    placed = place is not None
    return pl.pallas_call(
        unread(len(after), placed + n_in + 1, partial(out_kernel, n_in, n_out, placed)),
        out_shape=shapes,
        in_specs=[pl.BlockSpec(memory_space=pltpu.SMEM)] * placed + in_vmem(n_in + 1 + len(after)),
        out_specs=in_vmem(n_out),
        scratch_shapes=[pltpu.VMEM((total, depth), jnp.bfloat16)],
        compiler_params=pltpu.CompilerParams(vmem_limit_bytes=VMEM_BYTES),
        cost_estimate=pl.CostEstimate(flops=STEP_FLOPS, bytes_accessed=1000, transcendentals=0),
        name="project_out",
    )(*([place] if placed else []), *blocks, weight, *after)


def pick_kernel(parts, slots, order, spot, tokens, out):
    size = out.shape[2]
    for s in range(slots):
        for h in range(parts):
            pltpu.sync_copy(tokens.at[order[0, spot[0] * slots + s], pl.ds(h * size, size)], out.at[h, s])


def pick_samples(tokens, order, spot, slots, parts):
    _, seq, width = tokens.shape
    smem = pl.BlockSpec(memory_space=pltpu.SMEM)
    return pl.pallas_call(
        partial(pick_kernel, parts, slots),
        out_shape=jax.ShapeDtypeStruct((parts, slots, seq // parts, width), tokens.dtype),
        in_specs=[smem, smem, pl.BlockSpec(memory_space=pl.ANY)],
        out_specs=pl.BlockSpec(memory_space=pltpu.VMEM),
        compiler_params=pltpu.CompilerParams(vmem_limit_bytes=VMEM_BYTES),
        name="pick_samples",
    )(order, spot, tokens)


def layout_kernel(slots, spot, order, boundary, skip_offset, doc_lengths, frequency, _, angle, mask):
    seq, docs = mask.shape[1], doc_lengths.shape[1]
    for s in range(slots):
        sample = order[0, spot[0] * slots + s]
        place = lax.broadcasted_iota(jnp.int32, (seq, HEAD_DIM), 0)
        position = jnp.where(place < boundary[sample], place, place + skip_offset[sample])
        angle[s] = position.astype(jnp.float32) * frequency[...]
        row = lax.broadcasted_iota(jnp.int32, (seq, seq), 0)
        column = lax.broadcasted_iota(jnp.int32, (seq, seq), 1)
        row_doc, column_doc = jnp.zeros_like(row), jnp.zeros_like(row)
        end = jnp.int32(0)
        for k in range(docs):
            end = end + doc_lengths[sample, k]
            row_doc = row_doc + (row >= end).astype(jnp.int32)
            column_doc = column_doc + (column >= end).astype(jnp.int32)
        mask[s] = jnp.where((row_doc == column_doc) & (column <= row), 0.0, -jnp.inf)


def layout_of(order, boundary, skip_offset, doc_lengths, spot, slots, seq_len, after):
    half_dim = HEAD_DIM // 2
    exponent = jnp.arange(half_dim, dtype=jnp.float32) * (2.0 / HEAD_DIM)
    frequency = jnp.float32(ROPE_THETA) ** (-exponent)
    frequency = jnp.concatenate([frequency, frequency])[None]
    smem = pl.BlockSpec(memory_space=pltpu.SMEM)
    angle, mask = pl.pallas_call(
        partial(layout_kernel, slots),
        out_shape=[
            jax.ShapeDtypeStruct((slots, seq_len, HEAD_DIM), jnp.float32),
            jax.ShapeDtypeStruct((slots, seq_len, seq_len), jnp.float32),
        ],
        in_specs=[smem] * 5 + in_vmem(2),
        out_specs=in_vmem(2),
        compiler_params=pltpu.CompilerParams(vmem_limit_bytes=VMEM_BYTES),
        name="layout",
    )(spot, order, boundary, skip_offset, doc_lengths, frequency, after)
    sign = jnp.where(jnp.arange(HEAD_DIM) < half_dim, -1.0, 1.0).astype(jnp.float32)
    return jnp.cos(angle), jnp.sin(angle) * sign, mask


def swapped(value, axis, by):
    return lax.ppermute(value, axis, [(i, i ^ by) for i in range(lax.axis_size(axis))])


def partners(axis, peers):
    others = range(1, peers)
    return [0, *(others if axis == "dp" else reversed(others))]


def gather_blocks(block, axis, peers):
    return [block] + [swapped(block, axis, m) for m in partners(axis, peers)[1:]]


def trade_blocks(blocks, axis):
    order = partners(axis, len(blocks))
    return [blocks[0]] + [swapped(block, axis, m) for block, m in zip(blocks[1:], order[1:])]


def total_of(blocks):
    value = blocks[0].astype(jnp.float32)
    for block in blocks[1:]:
        value = value + block.astype(jnp.float32)
    return value


def steps_of(parts, layers):
    if parts == 1:
        return [(step, 0, number) for number in range(layers) for step in range(3)]
    steps = [(0, 0, 0), (1, 0, 0), (0, 1, 0), (2, 0, 0), (1, 1, 0)]
    for number in range(1, layers):
        steps += [(0, 0, number), (2, 1, number - 1), (1, 0, number), (0, 1, number), (2, 0, number), (1, 1, number)]
    return steps + [(2, 1, layers - 1)]


def per_device(
    tokens,
    w_query,
    w_key,
    w_value,
    w_out,
    norm_gain,
    boundary,
    skip_offset,
    doc_lengths,
    batch_order,
):
    replicas, sections, groups = lax.axis_size("dp"), lax.axis_size("pipe"), lax.axis_size("tensor")
    my_replica, my_section, my_group = lax.axis_index("dp"), lax.axis_index("pipe"), lax.axis_index("tensor")
    micro_count, seq_len, local_width = tokens.shape
    model_width = local_width * groups
    slots = micro_count // sections
    rows = slots * seq_len
    depth = w_query.shape[2]
    q_heads = w_query.shape[3] // HEAD_DIM
    kv_heads = w_key.shape[3] // HEAD_DIM
    paired = replicas == groups and replicas & (replicas - 1) == 0

    spot = jnp.reshape(my_section, (1,)).astype(jnp.int32)
    parts = 2 if paired else 1
    part_len = seq_len // parts
    stream = pick_samples(tokens, batch_order, spot, slots, parts).reshape(rows, local_width)

    gain_rows = lax.dynamic_slice_in_dim(norm_gain, my_replica * depth, depth, 2)
    held = (w_query, w_key, w_value, w_out)
    if sections == 2:
        gain_traded = swapped(gain_rows, "pipe", 1)
        gain_traded, held = lax.optimization_barrier((gain_traded, held))
        held = (gain_rows, *held)
        traded = [gain_traded] + [swapped(w, "pipe", 1) for w in held[1:]]

        def layer_weights(index, section):
            return [
                jnp.where(my_section == section, mine[index, 0], theirs[index, 0])
                for mine, theirs in zip(held, traded)
            ]
    else:
        gathered = [lax.all_gather(w, "pipe", axis=1, tiled=True) for w in (gain_rows, *held)]

        def layer_weights(index, section):
            return [w[index, section] for w in gathered]

    turn = [(i * groups + j, j * groups + i) for i in range(replicas) for j in range(groups)]
    if paired:
        base = lax.bitwise_xor(my_replica, my_group)
        place = lax.bitwise_xor(jnp.asarray(partners("tensor", groups), jnp.int32), base)
        place_out = lax.rem(groups - lax.bitwise_xor(jnp.arange(replicas, dtype=jnp.int32), base), groups)
        blocks = gather_blocks(lax.ppermute(stream, ("dp", "tensor"), turn), "tensor", groups)
    else:
        place = place_out = jnp.zeros((1,), jnp.int32)
        wide = lax.all_gather(stream, "tensor", axis=1, tiled=True)
        blocks = [lax.all_to_all(wide, "dp", split_axis=1, concat_axis=0, tiled=True)]
    part_rows = slots * part_len
    total = replicas * part_rows

    layers = [(0, s) for s in range(sections)] + [(1, s) for s in reversed(range(sections))]
    weights = [layer_weights(*layer) for layer in layers]
    streams, sums, mixed, shares = ([None] * parts for _ in range(4))
    before = [[] for _ in layers]
    layout, latest = None, []

    def share_out(h, number):
        nonlocal layout, latest
        gain, wq, wk, wv, _ = weights[number]
        head, arrays, part = (streams[h], shares[h], None) if number else (place, blocks, h)
        streams[h], ends = project_qkv(
            head, arrays, part, total, gain[None], wq, wk, wv, replicas if paired else 1, latest
        )
        latest = [streams[h]]
        if layout is None:
            layout = layout_of(batch_order, boundary, skip_offset, doc_lengths, spot, slots, seq_len, ends[0])
        if paired:
            sums[h] = trade_blocks(ends, "dp")
        else:
            pieces = ends[0].reshape(replicas, part_rows, ends[0].shape[1])
            pieces = lax.all_to_all(pieces, "dp", split_axis=0, concat_axis=0)
            sums[h] = [jnp.sum(pieces.astype(jnp.float32), axis=0)]

    def mix(h, number):
        nonlocal latest
        rows_out, keys, values = attend(
            sums[h], before[number], *layout, q_heads, kv_heads, model_width, latest
        )
        latest = [keys]
        before[number].append((keys, values))
        if paired:
            mixed[h] = gather_blocks(rows_out, "dp", replicas)
        else:
            mixed[h] = [lax.all_gather(rows_out, "dp", axis=0, tiled=True)]

    def bring_in(h, number):
        nonlocal latest
        last = number + 1 == len(layers)
        ends = project_out(
            mixed[h],
            place_out if paired and last else None,
            weights[number][4],
            groups if paired and last else 1,
            latest,
        )
        latest = ends[:1]
        if not paired:
            shares[h] = [lax.psum(ends[0].astype(jnp.float32), "tensor")]
        elif last:
            shares[h] = trade_blocks(ends, "tensor")
        else:
            shares[h] = gather_blocks(ends[0], "tensor", groups)

    for step, h, number in steps_of(parts, len(layers)):
        (share_out, mix, bring_in)[step](h, number)

    final = []
    for stream, share in zip(streams, shares):
        share = total_of(share)
        if paired:
            stream = lax.dynamic_slice_in_dim(stream, place[0] * part_rows, part_rows, 0)
            stream = (stream.astype(jnp.float32) + share).astype(jnp.bfloat16)
            stream = lax.ppermute(stream, ("dp", "tensor"), turn)
        else:
            stream = (stream.astype(jnp.float32) + share).astype(jnp.bfloat16)
            stream = lax.all_to_all(stream, "dp", split_axis=0, concat_axis=1, tiled=True)
            stream = lax.dynamic_slice_in_dim(stream, my_group * local_width, local_width, 1)
        final.append(stream.reshape(slots, part_len, local_width))
    if parts == sections == 2:
        first = my_section == 0
        came = swapped(jnp.where(first, final[1], final[0]), "pipe", 1)
        kept = jnp.where(first, final[0], final[1])
        return jnp.concatenate([jnp.where(first, kept, came), jnp.where(first, came, kept)], axis=0)
    final = jnp.concatenate(final, axis=1)
    return lax.all_to_all(final, "pipe", split_axis=1, concat_axis=0, tiled=True)


def solution(mesh):
    placed = (
        P("dp", None, "tensor"),
        P(None, "pipe", "dp", "tensor"),
        P(None, "pipe", "dp", "tensor"),
        P(None, "pipe", "dp", "tensor"),
        P(None, "pipe", "tensor", "dp"),
        P(None, "pipe", None),
        P("dp"),
        P("dp"),
        P("dp", None),
        P("dp", None),
    )
    return jax.shard_map(
        per_device, mesh=mesh, in_specs=placed, out_specs=P("dp", "pipe", "tensor"), check_vma=False
    )
```

```python
from functools import partial

import jax
import jax.numpy as jnp
from jax import lax
from jax.experimental import pallas as pl
from jax.experimental.pallas import tpu as pltpu
from jax.sharding import PartitionSpec as P

HEAD_DIM = 128
LANES = 128
STAT_ROWS = 16
ROPE_THETA = 500000.0
NORM_EPSILON = 1e-05
VMEM_BYTES = 8 * 1024 * 1024
STEP_FLOPS = 5_500_000_000


def unread(count, at, kernel):
    def wrapped(*refs):
        return kernel(*refs[:at], *refs[at + count :])

    return wrapped


def in_vmem(count):
    return [pl.BlockSpec(memory_space=pltpu.VMEM)] * count


def column_tiles(width, tile):
    return [(at, min(tile, width - at)) for at in range(0, width, tile)]


def diagonal(rows, offset):
    row = lax.broadcasted_iota(jnp.int32, (rows, LANES), 0)
    return row + offset == lax.broadcasted_iota(jnp.int32, (rows, LANES), 1)


def qkv_kernel(n_in, n_out, part, *refs):
    if part is None:
        so_far, *shares = refs[: 1 + n_in]
    else:
        place, *blocks = refs[: 1 + n_in]
    gain, wq, wk, wv, stream = refs[1 + n_in : 6 + n_in]
    outs, (rows,) = refs[6 + n_in : 6 + n_in + n_out], refs[6 + n_in + n_out :]
    scale = gain[...]
    if part is None:
        sums = [share[...].astype(jnp.float32) for share in shares]
        while len(sums) > 1:
            sums = [sums[m] + sums[m + 1] if m + 1 < len(sums) else sums[m] for m in range(0, len(sums), 2)]
        stream[...] = (so_far[...].astype(jnp.float32) + sums[0]).astype(stream.dtype)
    else:
        size = stream.shape[0] // n_in
        for m, block in enumerate(blocks):
            at = pl.ds(pl.multiple_of(place[m] * size, size), size)
            stream[at, :] = block[part * size : (part + 1) * size]
    wide = stream[...].astype(jnp.float32)
    rows[...] = (wide * scale).astype(jnp.bfloat16)
    total = jnp.sum(wide * wide, axis=-1, keepdims=True)
    size = rows.shape[0] // n_out
    start = 0
    for weight in (wq, wk, wv):
        for at, width in column_tiles(weight.shape[1], 512):
            product = jnp.dot(rows[...], weight[:, at : at + width], preferred_element_type=jnp.float32)
            for m, out in enumerate(outs):
                for lane in range(0, width, LANES):
                    piece = product[m * size : (m + 1) * size, lane : lane + LANES]
                    out[pl.ds((start + at + lane) // LANES * size, size), :] = piece.astype(out.dtype)
        start += weight.shape[1]
    base = start // LANES * size
    for m, out in enumerate(outs):
        for k, at in enumerate(range(0, size, LANES)):
            part_total = total[m * size + at : m * size + min(at + LANES, size)]
            lying = jnp.sum(jnp.where(diagonal(part_total.shape[0], 0), part_total, 0.0), axis=0, keepdims=True)
            high = lying.astype(jnp.bfloat16).astype(jnp.float32)
            line = lax.broadcasted_iota(jnp.int32, (STAT_ROWS, LANES), 0)
            tile = jnp.where(line == 0, high, jnp.where(line == 1, lying - high, 0.0))
            out[pl.ds(base + k * STAT_ROWS, STAT_ROWS), :] = tile.astype(out.dtype)


def project_qkv(head, arrays, part, total, gain, wq, wk, wv, n_out, after):
    depth = wq.shape[0]
    size = total // n_out
    height = (wq.shape[1] + wk.shape[1] + wv.shape[1]) // LANES * size + -(-size // LANES) * STAT_ROWS
    shapes = [jax.ShapeDtypeStruct((total, depth), jnp.bfloat16)] + [
        jax.ShapeDtypeStruct((height, LANES), jnp.float32 if m == 0 and n_out > 1 else jnp.bfloat16)
        for m in range(n_out)
    ]
    first = in_vmem(1) if part is None else [pl.BlockSpec(memory_space=pltpu.SMEM)]
    stream, *sums = pl.pallas_call(
        unread(len(after), len(arrays) + 5, partial(qkv_kernel, len(arrays), n_out, part)),
        out_shape=shapes,
        in_specs=first + in_vmem(len(arrays) + 4 + len(after)),
        out_specs=in_vmem(1 + n_out),
        scratch_shapes=[pltpu.VMEM((total, depth), jnp.bfloat16)],
        compiler_params=pltpu.CompilerParams(vmem_limit_bytes=VMEM_BYTES),
        cost_estimate=pl.CostEstimate(flops=STEP_FLOPS, bytes_accessed=1000, transcendentals=0),
        name="project_qkv",
    )(head, *arrays, gain, wq, wk, wv, *after)
    return stream, sums


def attention_kernel(n_in, n_before, q_heads, kv_heads, model_width, *refs):
    blocks, before, refs = refs[:n_in], refs[n_in : n_in + 2 * n_before], refs[n_in + 2 * n_before :]
    cosine, sine, mask, out, key_out, value_out = refs
    samples = cosine.shape[0]
    size = out.shape[0] // samples
    group = q_heads // kv_heads
    first = n_before * size

    def summed(at, height):
        value = blocks[0][at : at + height].astype(jnp.float32)
        for block in blocks[1:]:
            value = value + block[at : at + height].astype(jnp.float32)
        return value

    k_at, v_at = q_heads, q_heads + kv_heads
    s_at = (q_heads + 2 * kv_heads) * out.shape[0]
    for s in range(samples):
        rows = slice(s * size, (s + 1) * size)
        tile = summed(s_at + s * size // LANES * STAT_ROWS, STAT_ROWS)
        lying = jnp.broadcast_to(tile[:1] + tile[1:2], (size, LANES))
        squares = jnp.sum(jnp.where(diagonal(size, s * size % LANES), lying, 0.0), axis=-1, keepdims=True)
        inverse = lax.rsqrt(squares * (1.0 / model_width) + NORM_EPSILON)
        cos, sin = cosine[s, first : first + size], sine[s, first : first + size]
        bias = mask[s, first : first + size, : first + size]

        def head(at):
            return summed(at * out.shape[0] + s * size, size) * inverse

        def rotated(at):
            value = head(at)
            turned = pltpu.roll(value, HEAD_DIM // 2, 1)
            return (value * cos + turned * sin).astype(jnp.bfloat16)

        bias_all = jnp.concatenate([bias] * group, axis=0)
        for kv in range(kv_heads):
            lanes = slice(kv * HEAD_DIM, (kv + 1) * HEAD_DIM)
            key = rotated(k_at + kv)
            value = head(v_at + kv).astype(jnp.bfloat16)
            key_out[rows, lanes] = key
            value_out[rows, lanes] = value
            if n_before:
                key = jnp.concatenate([k[rows, lanes] for k in before[0::2]] + [key], axis=0)
                value = jnp.concatenate([v[rows, lanes] for v in before[1::2]] + [value], axis=0)
            query = jnp.concatenate([rotated(kv * group + g) for g in range(group)], axis=0)
            scores = lax.dot_general(query, key, (((1,), (1,)), ((), ())), preferred_element_type=jnp.float32)
            scores = scores * HEAD_DIM ** (-0.5) + bias_all
            top = jnp.max(scores, axis=-1, keepdims=True)
            weights = jnp.exp(scores - top)
            weights = weights / jnp.sum(weights, axis=-1, keepdims=True)
            mixed = jnp.dot(weights.astype(jnp.bfloat16), value, preferred_element_type=jnp.float32)
            for g in range(group):
                at = (kv * group + g) * HEAD_DIM
                out[rows, at : at + HEAD_DIM] = mixed[g * size : (g + 1) * size].astype(out.dtype)


def attend(rows, blocks, before, cosine, sine, mask, q_heads, kv_heads, model_width, after):
    shapes = [(rows, heads * HEAD_DIM) for heads in (q_heads, kv_heads, kv_heads)]
    return pl.pallas_call(
        unread(
            len(after),
            len(blocks) + 2 * len(before) + 3,
            partial(attention_kernel, len(blocks), len(before), q_heads, kv_heads, model_width),
        ),
        out_shape=[jax.ShapeDtypeStruct(shape, jnp.bfloat16) for shape in shapes],
        in_specs=in_vmem(len(blocks) + 2 * len(before) + 3 + len(after)),
        out_specs=in_vmem(3),
        compiler_params=pltpu.CompilerParams(vmem_limit_bytes=VMEM_BYTES),
        cost_estimate=pl.CostEstimate(flops=STEP_FLOPS, bytes_accessed=1000, transcendentals=0),
        name="attend",
    )(*blocks, *[array for pair in before for array in pair], cosine, sine, mask, *after)


def out_kernel(n_in, n_out, placed, *refs):
    place, refs = (refs[0], refs[1:]) if placed else (None, refs)
    blocks, weight = refs[:n_in], refs[n_in]
    outs, (rows,) = refs[n_in + 1 : n_in + 1 + n_out], refs[n_in + 1 + n_out :]
    size = blocks[0].shape[0]
    for m, block in enumerate(blocks):
        at = pl.multiple_of(place[m] * size, size) if placed else m * size
        rows[pl.ds(at, size), :] = block[...]
    out_size = outs[0].shape[0]
    for at, width in column_tiles(weight.shape[1], 512):
        product = jnp.dot(rows[...], weight[:, at : at + width], preferred_element_type=jnp.float32)
        for m, out in enumerate(outs):
            out[:, at : at + width] = product[m * out_size : (m + 1) * out_size].astype(out.dtype)


def project_out(blocks, place, weight, n_out, after):
    n_in = len(blocks)
    total = n_in * blocks[0].shape[0]
    depth, columns = weight.shape
    shapes = [
        jax.ShapeDtypeStruct((total // n_out, columns), jnp.float32 if m == 0 and n_out > 1 else jnp.bfloat16)
        for m in range(n_out)
    ]
    placed = place is not None
    return pl.pallas_call(
        unread(len(after), placed + n_in + 1, partial(out_kernel, n_in, n_out, placed)),
        out_shape=shapes,
        in_specs=[pl.BlockSpec(memory_space=pltpu.SMEM)] * placed + in_vmem(n_in + 1 + len(after)),
        out_specs=in_vmem(n_out),
        scratch_shapes=[pltpu.VMEM((total, depth), jnp.bfloat16)],
        compiler_params=pltpu.CompilerParams(vmem_limit_bytes=VMEM_BYTES),
        cost_estimate=pl.CostEstimate(flops=STEP_FLOPS, bytes_accessed=1000, transcendentals=0),
        name="project_out",
    )(*([place] if placed else []), *blocks, weight, *after)


def pick_kernel(parts, slots, order, spot, tokens, out):
    size = out.shape[2]
    for s in range(slots):
        for h in range(parts):
            pltpu.sync_copy(tokens.at[order[0, spot[0] * slots + s], pl.ds(h * size, size)], out.at[h, s])


def pick_samples(tokens, order, spot, slots, parts):
    _, seq, width = tokens.shape
    smem = pl.BlockSpec(memory_space=pltpu.SMEM)
    return pl.pallas_call(
        partial(pick_kernel, parts, slots),
        out_shape=jax.ShapeDtypeStruct((parts, slots, seq // parts, width), tokens.dtype),
        in_specs=[smem, smem, pl.BlockSpec(memory_space=pl.ANY)],
        out_specs=pl.BlockSpec(memory_space=pltpu.VMEM),
        compiler_params=pltpu.CompilerParams(vmem_limit_bytes=VMEM_BYTES),
        name="pick_samples",
    )(order, spot, tokens)


def layout_kernel(slots, spot, order, boundary, skip_offset, doc_lengths, frequency, _, angle, mask):
    seq, docs = mask.shape[1], doc_lengths.shape[1]
    for s in range(slots):
        sample = order[0, spot[0] * slots + s]
        place = lax.broadcasted_iota(jnp.int32, (seq, HEAD_DIM), 0)
        position = jnp.where(place < boundary[sample], place, place + skip_offset[sample])
        angle[s] = position.astype(jnp.float32) * frequency[...]
        row = lax.broadcasted_iota(jnp.int32, (seq, seq), 0)
        column = lax.broadcasted_iota(jnp.int32, (seq, seq), 1)
        row_doc, column_doc = jnp.zeros_like(row), jnp.zeros_like(row)
        end = jnp.int32(0)
        for k in range(docs):
            end = end + doc_lengths[sample, k]
            row_doc = row_doc + (row >= end).astype(jnp.int32)
            column_doc = column_doc + (column >= end).astype(jnp.int32)
        mask[s] = jnp.where((row_doc == column_doc) & (column <= row), 0.0, -jnp.inf)


def layout_of(order, boundary, skip_offset, doc_lengths, spot, slots, seq_len, after):
    half_dim = HEAD_DIM // 2
    exponent = jnp.arange(half_dim, dtype=jnp.float32) * (2.0 / HEAD_DIM)
    frequency = jnp.float32(ROPE_THETA) ** (-exponent)
    frequency = jnp.concatenate([frequency, frequency])[None]
    smem = pl.BlockSpec(memory_space=pltpu.SMEM)
    angle, mask = pl.pallas_call(
        partial(layout_kernel, slots),
        out_shape=[
            jax.ShapeDtypeStruct((slots, seq_len, HEAD_DIM), jnp.float32),
            jax.ShapeDtypeStruct((slots, seq_len, seq_len), jnp.float32),
        ],
        in_specs=[smem] * 5 + in_vmem(2),
        out_specs=in_vmem(2),
        compiler_params=pltpu.CompilerParams(vmem_limit_bytes=VMEM_BYTES),
        name="layout",
    )(spot, order, boundary, skip_offset, doc_lengths, frequency, after)
    sign = jnp.where(jnp.arange(HEAD_DIM) < half_dim, -1.0, 1.0).astype(jnp.float32)
    return jnp.cos(angle), jnp.sin(angle) * sign, mask


def swapped(value, axis, by):
    return lax.ppermute(value, axis, [(i, i ^ by) for i in range(lax.axis_size(axis))])


def partners(axis, peers):
    others = range(1, peers)
    return [0, *(others if axis == "dp" else reversed(others))]


def gather_blocks(block, axis, peers):
    return [block] + [swapped(block, axis, m) for m in partners(axis, peers)[1:]]


def trade_blocks(blocks, axis):
    order = partners(axis, len(blocks))
    return [blocks[0]] + [swapped(block, axis, m) for block, m in zip(blocks[1:], order[1:])]


def total_of(blocks):
    value = blocks[0].astype(jnp.float32)
    for block in blocks[1:]:
        value = value + block.astype(jnp.float32)
    return value


def steps_of(parts, layers):
    if parts == 1:
        return [(step, 0, number) for number in range(layers) for step in range(3)]
    steps = [(0, 0, 0), (1, 0, 0), (0, 1, 0), (2, 0, 0), (1, 1, 0)]
    for number in range(1, layers):
        steps += [(0, 0, number), (2, 1, number - 1), (1, 0, number), (0, 1, number), (2, 0, number), (1, 1, number)]
    return steps + [(2, 1, layers - 1)]


def per_device(
    tokens,
    w_query,
    w_key,
    w_value,
    w_out,
    norm_gain,
    boundary,
    skip_offset,
    doc_lengths,
    batch_order,
):
    replicas, sections, groups = lax.axis_size("dp"), lax.axis_size("pipe"), lax.axis_size("tensor")
    my_replica, my_section, my_group = lax.axis_index("dp"), lax.axis_index("pipe"), lax.axis_index("tensor")
    micro_count, seq_len, local_width = tokens.shape
    model_width = local_width * groups
    slots = micro_count // sections
    rows = slots * seq_len
    depth = w_query.shape[2]
    q_heads = w_query.shape[3] // HEAD_DIM
    kv_heads = w_key.shape[3] // HEAD_DIM
    paired = replicas == groups and replicas & (replicas - 1) == 0

    spot = jnp.reshape(my_section, (1,)).astype(jnp.int32)
    parts = 2 if paired else 1
    part_len = seq_len // parts
    stream = pick_samples(tokens, batch_order, spot, slots, parts).reshape(rows, local_width)

    gain_rows = lax.dynamic_slice_in_dim(norm_gain, my_replica * depth, depth, 2)
    held = (w_query, w_key, w_value, w_out)
    if sections == 2:
        gain_traded = swapped(gain_rows, "pipe", 1)
        gain_traded, held = lax.optimization_barrier((gain_traded, held))
        held = (gain_rows, *held)
        traded = [gain_traded] + [swapped(w, "pipe", 1) for w in held[1:]]

        def layer_weights(index, section):
            return [
                jnp.where(my_section == section, mine[index, 0], theirs[index, 0])
                for mine, theirs in zip(held, traded)
            ]
    else:
        gathered = [lax.all_gather(w, "pipe", axis=1, tiled=True) for w in (gain_rows, *held)]

        def layer_weights(index, section):
            return [w[index, section] for w in gathered]

    turn = [(i * groups + j, j * groups + i) for i in range(replicas) for j in range(groups)]
    if paired:
        base = lax.bitwise_xor(my_replica, my_group)
        place = lax.bitwise_xor(jnp.asarray(partners("tensor", groups), jnp.int32), base)
        place_out = lax.rem(groups - lax.bitwise_xor(jnp.arange(replicas, dtype=jnp.int32), base), groups)
        blocks = gather_blocks(lax.ppermute(stream, ("dp", "tensor"), turn), "tensor", groups)
    else:
        place = place_out = jnp.zeros((1,), jnp.int32)
        wide = lax.all_gather(stream, "tensor", axis=1, tiled=True)
        blocks = [lax.all_to_all(wide, "dp", split_axis=1, concat_axis=0, tiled=True)]
    part_rows = slots * part_len
    total = replicas * part_rows

    layers = [(0, s) for s in range(sections)] + [(1, s) for s in reversed(range(sections))]
    weights = [layer_weights(*layer) for layer in layers]
    streams, sums, mixed, shares = ([None] * parts for _ in range(4))
    before = [[] for _ in layers]
    layout, latest = None, []

    def share_out(h, number):
        nonlocal layout, latest
        gain, wq, wk, wv, _ = weights[number]
        head, arrays, part = (streams[h], shares[h], None) if number else (place, blocks, h)
        streams[h], ends = project_qkv(
            head, arrays, part, total, gain[None], wq, wk, wv, replicas, latest
        )
        latest = [streams[h]]
        if layout is None:
            layout = layout_of(batch_order, boundary, skip_offset, doc_lengths, spot, slots, seq_len, ends[0])
        if paired:
            sums[h] = trade_blocks(ends, "dp")
        else:
            pieces = jnp.stack([end.astype(jnp.bfloat16) for end in ends])
            pieces = lax.all_to_all(pieces, "dp", split_axis=0, concat_axis=0)
            sums[h] = [jnp.sum(pieces.astype(jnp.float32), axis=0)]

    def mix(h, number):
        nonlocal latest
        rows_out, keys, values = attend(
            part_rows, sums[h], before[number], *layout, q_heads, kv_heads, model_width, latest
        )
        latest = [keys]
        before[number].append((keys, values))
        if paired:
            mixed[h] = gather_blocks(rows_out, "dp", replicas)
        else:
            mixed[h] = [lax.all_gather(rows_out, "dp", axis=0, tiled=True)]

    def bring_in(h, number):
        nonlocal latest
        last = number + 1 == len(layers)
        ends = project_out(
            mixed[h],
            place_out if paired and last else None,
            weights[number][4],
            groups if paired and last else 1,
            latest,
        )
        latest = ends[:1]
        if not paired:
            shares[h] = [lax.psum(ends[0].astype(jnp.float32), "tensor")]
        elif last:
            shares[h] = trade_blocks(ends, "tensor")
        else:
            shares[h] = gather_blocks(ends[0], "tensor", groups)

    for step, h, number in steps_of(parts, len(layers)):
        (share_out, mix, bring_in)[step](h, number)

    final = []
    for stream, share in zip(streams, shares):
        share = total_of(share)
        if paired:
            stream = lax.dynamic_slice_in_dim(stream, place[0] * part_rows, part_rows, 0)
            stream = (stream.astype(jnp.float32) + share).astype(jnp.bfloat16)
            stream = lax.ppermute(stream, ("dp", "tensor"), turn)
        else:
            stream = (stream.astype(jnp.float32) + share).astype(jnp.bfloat16)
            stream = lax.all_to_all(stream, "dp", split_axis=0, concat_axis=1, tiled=True)
            stream = lax.dynamic_slice_in_dim(stream, my_group * local_width, local_width, 1)
        final.append(stream.reshape(slots, part_len, local_width))
    if parts == sections == 2:
        first = my_section == 0
        came = swapped(jnp.where(first, final[1], final[0]), "pipe", 1)
        kept = jnp.where(first, final[0], final[1])
        return jnp.concatenate([jnp.where(first, kept, came), jnp.where(first, came, kept)], axis=0)
    final = jnp.concatenate(final, axis=1)
    return lax.all_to_all(final, "pipe", split_axis=1, concat_axis=0, tiled=True)


def solution(mesh):
    placed = (
        P("dp", None, "tensor"),
        P(None, "pipe", "dp", "tensor"),
        P(None, "pipe", "dp", "tensor"),
        P(None, "pipe", "dp", "tensor"),
        P(None, "pipe", "tensor", "dp"),
        P(None, "pipe", None),
        P("dp"),
        P("dp"),
        P("dp", None),
        P("dp", None),
    )
    return jax.shard_map(
        per_device, mesh=mesh, in_specs=placed, out_specs=P("dp", "pipe", "tensor"), check_vma=False
    )
```

```python
from functools import partial

import jax
import jax.numpy as jnp
from jax import lax
from jax.experimental import pallas as pl
from jax.experimental.pallas import tpu as pltpu
from jax.sharding import PartitionSpec as P

HEAD_DIM = 128
LANES = 128
STAT_ROWS = 16
ROPE_THETA = 500000.0
NORM_EPSILON = 1e-05
VMEM_BYTES = 8 * 1024 * 1024
STEP_FLOPS = 5_500_000_000


def unread(count, at, kernel):
    def wrapped(*refs):
        return kernel(*refs[:at], *refs[at + count :])

    return wrapped


def in_vmem(count):
    return [pl.BlockSpec(memory_space=pltpu.VMEM)] * count


def column_tiles(width, tile):
    return [(at, min(tile, width - at)) for at in range(0, width, tile)]


def diagonal(rows, offset):
    row = lax.broadcasted_iota(jnp.int32, (rows, LANES), 0)
    return row + offset == lax.broadcasted_iota(jnp.int32, (rows, LANES), 1)


def qkv_kernel(n_in, n_out, part, *refs):
    if part is None:
        so_far, *shares = refs[: 1 + n_in]
    else:
        place, *blocks = refs[: 1 + n_in]
    gain, wq, wk, wv, stream = refs[1 + n_in : 6 + n_in]
    outs, (rows,) = refs[6 + n_in : 6 + n_in + n_out], refs[6 + n_in + n_out :]
    scale = gain[...]
    if part is None:
        sums = [share[...].astype(jnp.float32) for share in shares]
        while len(sums) > 1:
            sums = [sums[m] + sums[m + 1] if m + 1 < len(sums) else sums[m] for m in range(0, len(sums), 2)]
        stream[...] = (so_far[...].astype(jnp.float32) + sums[0]).astype(stream.dtype)
    else:
        size = stream.shape[0] // n_in
        for m, block in enumerate(blocks):
            at = pl.ds(pl.multiple_of(place[m] * size, size), size)
            stream[at, :] = block[part * size : (part + 1) * size]
    wide = stream[...].astype(jnp.float32)
    rows[...] = (wide * scale).astype(jnp.bfloat16)
    total = jnp.sum(wide * wide, axis=-1, keepdims=True)
    size = rows.shape[0] // n_out
    start = 0
    for weight in (wq, wk, wv):
        for at, width in column_tiles(weight.shape[1], 512):
            product = jnp.dot(rows[...], weight[:, at : at + width], preferred_element_type=jnp.float32)
            for m, out in enumerate(outs):
                for lane in range(0, width, LANES):
                    piece = product[m * size : (m + 1) * size, lane : lane + LANES]
                    out[pl.ds((start + at + lane) // LANES * size, size), :] = piece.astype(out.dtype)
        start += weight.shape[1]
    base = start // LANES * size
    for m, out in enumerate(outs):
        for k, at in enumerate(range(0, size, LANES)):
            part_total = total[m * size + at : m * size + min(at + LANES, size)]
            lying = jnp.sum(jnp.where(diagonal(part_total.shape[0], 0), part_total, 0.0), axis=0, keepdims=True)
            high = lying.astype(jnp.bfloat16).astype(jnp.float32)
            line = lax.broadcasted_iota(jnp.int32, (STAT_ROWS, LANES), 0)
            tile = jnp.where(line == 0, high, jnp.where(line == 1, lying - high, 0.0))
            out[pl.ds(base + k * STAT_ROWS, STAT_ROWS), :] = tile.astype(out.dtype)


def project_qkv(head, arrays, part, total, gain, wq, wk, wv, n_out, after):
    depth = wq.shape[0]
    size = total // n_out
    height = (wq.shape[1] + wk.shape[1] + wv.shape[1]) // LANES * size + -(-size // LANES) * STAT_ROWS
    shapes = [jax.ShapeDtypeStruct((total, depth), jnp.bfloat16)] + [
        jax.ShapeDtypeStruct((height, LANES), jnp.float32 if m == 0 and n_out > 1 else jnp.bfloat16)
        for m in range(n_out)
    ]
    first = in_vmem(1) if part is None else [pl.BlockSpec(memory_space=pltpu.SMEM)]
    stream, *sums = pl.pallas_call(
        unread(len(after), len(arrays) + 5, partial(qkv_kernel, len(arrays), n_out, part)),
        out_shape=shapes,
        in_specs=first + in_vmem(len(arrays) + 4 + len(after)),
        out_specs=in_vmem(1 + n_out),
        scratch_shapes=[pltpu.VMEM((total, depth), jnp.bfloat16)],
        compiler_params=pltpu.CompilerParams(vmem_limit_bytes=VMEM_BYTES),
        cost_estimate=pl.CostEstimate(flops=STEP_FLOPS, bytes_accessed=1000, transcendentals=0),
        name="project_qkv",
    )(head, *arrays, gain, wq, wk, wv, *after)
    return stream, sums


def attention_kernel(n_in, n_before, q_heads, kv_heads, model_width, *refs):
    blocks, before, refs = refs[:n_in], refs[n_in : n_in + 2 * n_before], refs[n_in + 2 * n_before :]
    cosine, sine, mask, out, key_out, value_out = refs
    samples = cosine.shape[0]
    size = out.shape[0] // samples
    group = q_heads // kv_heads
    first = n_before * size

    def summed(at, height):
        value = blocks[0][at : at + height].astype(jnp.float32)
        for block in blocks[1:]:
            value = value + block[at : at + height].astype(jnp.float32)
        return value

    k_at, v_at = q_heads, q_heads + kv_heads
    s_at = (q_heads + 2 * kv_heads) * out.shape[0]
    for s in range(samples):
        rows = slice(s * size, (s + 1) * size)
        tile = summed(s_at + s * size // LANES * STAT_ROWS, STAT_ROWS)
        lying = jnp.broadcast_to(tile[:1] + tile[1:2], (size, LANES))
        squares = jnp.sum(jnp.where(diagonal(size, s * size % LANES), lying, 0.0), axis=-1, keepdims=True)
        inverse = lax.rsqrt(squares * (1.0 / model_width) + NORM_EPSILON)
        cos, sin = cosine[s, first : first + size], sine[s, first : first + size]
        bias = mask[s, first : first + size, : first + size]

        def head(at):
            return summed(at * out.shape[0] + s * size, size) * inverse

        def rotated(at):
            value = head(at)
            turned = pltpu.roll(value, HEAD_DIM // 2, 1)
            return (value * cos + turned * sin).astype(jnp.bfloat16)

        bias_all = jnp.concatenate([bias] * group, axis=0)
        for kv in range(kv_heads):
            lanes = slice(kv * HEAD_DIM, (kv + 1) * HEAD_DIM)
            key = rotated(k_at + kv)
            value = head(v_at + kv).astype(jnp.bfloat16)
            key_out[rows, lanes] = key
            value_out[rows, lanes] = value
            if n_before:
                key = jnp.concatenate([k[rows, lanes] for k in before[0::2]] + [key], axis=0)
                value = jnp.concatenate([v[rows, lanes] for v in before[1::2]] + [value], axis=0)
            query = jnp.concatenate([rotated(kv * group + g) for g in range(group)], axis=0)
            scores = lax.dot_general(query, key, (((1,), (1,)), ((), ())), preferred_element_type=jnp.float32)
            scores = scores * HEAD_DIM ** (-0.5) + bias_all
            top = jnp.max(scores, axis=-1, keepdims=True)
            weights = jnp.exp(scores - top)
            weights = weights / jnp.sum(weights, axis=-1, keepdims=True)
            mixed = jnp.dot(weights.astype(jnp.bfloat16), value, preferred_element_type=jnp.float32)
            for g in range(group):
                at = (kv * group + g) * HEAD_DIM
                out[rows, at : at + HEAD_DIM] = mixed[g * size : (g + 1) * size].astype(out.dtype)


def attend(rows, blocks, before, cosine, sine, mask, q_heads, kv_heads, model_width, after):
    shapes = [(rows, heads * HEAD_DIM) for heads in (q_heads, kv_heads, kv_heads)]
    return pl.pallas_call(
        unread(
            len(after),
            len(blocks) + 2 * len(before) + 3,
            partial(attention_kernel, len(blocks), len(before), q_heads, kv_heads, model_width),
        ),
        out_shape=[jax.ShapeDtypeStruct(shape, jnp.bfloat16) for shape in shapes],
        in_specs=in_vmem(len(blocks) + 2 * len(before) + 3 + len(after)),
        out_specs=in_vmem(3),
        compiler_params=pltpu.CompilerParams(vmem_limit_bytes=VMEM_BYTES),
        cost_estimate=pl.CostEstimate(flops=STEP_FLOPS, bytes_accessed=1000, transcendentals=0),
        name="attend",
    )(*blocks, *[array for pair in before for array in pair], cosine, sine, mask, *after)


def out_kernel(n_in, n_out, placed, *refs):
    place, refs = (refs[0], refs[1:]) if placed else (None, refs)
    blocks, weight = refs[:n_in], refs[n_in]
    outs, (rows,) = refs[n_in + 1 : n_in + 1 + n_out], refs[n_in + 1 + n_out :]
    size = blocks[0].shape[0]
    for m, block in enumerate(blocks):
        at = pl.multiple_of(place[m] * size, size) if placed else m * size
        rows[pl.ds(at, size), :] = block[...]
    out_size = outs[0].shape[0]
    for at, width in column_tiles(weight.shape[1], 512):
        product = jnp.dot(rows[...], weight[:, at : at + width], preferred_element_type=jnp.float32)
        for m, out in enumerate(outs):
            out[:, at : at + width] = product[m * out_size : (m + 1) * out_size].astype(out.dtype)


def project_out(blocks, place, weight, n_out, after):
    n_in = len(blocks)
    total = n_in * blocks[0].shape[0]
    depth, columns = weight.shape
    shapes = [
        jax.ShapeDtypeStruct((total // n_out, columns), jnp.float32 if m == 0 and n_out > 1 else jnp.bfloat16)
        for m in range(n_out)
    ]
    placed = place is not None
    return pl.pallas_call(
        unread(len(after), placed + n_in + 1, partial(out_kernel, n_in, n_out, placed)),
        out_shape=shapes,
        in_specs=[pl.BlockSpec(memory_space=pltpu.SMEM)] * placed + in_vmem(n_in + 1 + len(after)),
        out_specs=in_vmem(n_out),
        scratch_shapes=[pltpu.VMEM((total, depth), jnp.bfloat16)],
        compiler_params=pltpu.CompilerParams(vmem_limit_bytes=VMEM_BYTES),
        cost_estimate=pl.CostEstimate(flops=STEP_FLOPS, bytes_accessed=1000, transcendentals=0),
        name="project_out",
    )(*([place] if placed else []), *blocks, weight, *after)


def pick_kernel(parts, slots, order, spot, tokens, out):
    size = out.shape[2]
    for s in range(slots):
        for h in range(parts):
            pltpu.sync_copy(tokens.at[order[0, spot[0] * slots + s], pl.ds(h * size, size)], out.at[h, s])


def pick_samples(tokens, order, spot, slots, parts):
    _, seq, width = tokens.shape
    smem = pl.BlockSpec(memory_space=pltpu.SMEM)
    return pl.pallas_call(
        partial(pick_kernel, parts, slots),
        out_shape=jax.ShapeDtypeStruct((parts, slots, seq // parts, width), tokens.dtype),
        in_specs=[smem, smem, pl.BlockSpec(memory_space=pl.ANY)],
        out_specs=pl.BlockSpec(memory_space=pltpu.VMEM),
        compiler_params=pltpu.CompilerParams(vmem_limit_bytes=VMEM_BYTES),
        name="pick_samples",
    )(order, spot, tokens)


def layout_kernel(slots, spot, order, boundary, skip_offset, doc_lengths, frequency, _, angle, mask):
    seq, docs = mask.shape[1], doc_lengths.shape[1]
    for s in range(slots):
        sample = order[0, spot[0] * slots + s]
        place = lax.broadcasted_iota(jnp.int32, (seq, HEAD_DIM), 0)
        position = jnp.where(place < boundary[sample], place, place + skip_offset[sample])
        angle[s] = position.astype(jnp.float32) * frequency[...]
        row = lax.broadcasted_iota(jnp.int32, (seq, seq), 0)
        column = lax.broadcasted_iota(jnp.int32, (seq, seq), 1)
        row_doc, column_doc = jnp.zeros_like(row), jnp.zeros_like(row)
        end = jnp.int32(0)
        for k in range(docs):
            end = end + doc_lengths[sample, k]
            row_doc = row_doc + (row >= end).astype(jnp.int32)
            column_doc = column_doc + (column >= end).astype(jnp.int32)
        mask[s] = jnp.where((row_doc == column_doc) & (column <= row), 0.0, -jnp.inf)


def layout_of(order, boundary, skip_offset, doc_lengths, spot, slots, seq_len, after):
    half_dim = HEAD_DIM // 2
    exponent = jnp.arange(half_dim, dtype=jnp.float32) * (2.0 / HEAD_DIM)
    frequency = jnp.float32(ROPE_THETA) ** (-exponent)
    frequency = jnp.concatenate([frequency, frequency])[None]
    smem = pl.BlockSpec(memory_space=pltpu.SMEM)
    angle, mask = pl.pallas_call(
        partial(layout_kernel, slots),
        out_shape=[
            jax.ShapeDtypeStruct((slots, seq_len, HEAD_DIM), jnp.float32),
            jax.ShapeDtypeStruct((slots, seq_len, seq_len), jnp.float32),
        ],
        in_specs=[smem] * 5 + in_vmem(2),
        out_specs=in_vmem(2),
        compiler_params=pltpu.CompilerParams(vmem_limit_bytes=VMEM_BYTES),
        name="layout",
    )(spot, order, boundary, skip_offset, doc_lengths, frequency, after)
    sign = jnp.where(jnp.arange(HEAD_DIM) < half_dim, -1.0, 1.0).astype(jnp.float32)
    return jnp.cos(angle), jnp.sin(angle) * sign, mask


def swapped(value, axis, by):
    return lax.ppermute(value, axis, [(i, i ^ by) for i in range(lax.axis_size(axis))])


def partners(axis, peers):
    others = range(1, peers)
    return [0, *(others if axis == "dp" else reversed(others))]


def gather_blocks(block, axis, peers):
    return [block] + [swapped(block, axis, m) for m in partners(axis, peers)[1:]]


def trade_blocks(blocks, axis):
    order = partners(axis, len(blocks))
    return [blocks[0]] + [swapped(block, axis, m) for block, m in zip(blocks[1:], order[1:])]


def total_of(blocks):
    value = blocks[0].astype(jnp.float32)
    for block in blocks[1:]:
        value = value + block.astype(jnp.float32)
    return value


def steps_of(parts, layers):
    if parts == 1:
        return [(step, 0, number) for number in range(layers) for step in range(3)]
    steps = [(0, 0, 0), (1, 0, 0), (0, 1, 0), (2, 0, 0), (1, 1, 0)]
    for number in range(1, layers):
        steps += [(0, 0, number), (2, 1, number - 1), (1, 0, number), (0, 1, number), (2, 0, number), (1, 1, number)]
    return steps + [(2, 1, layers - 1)]


def per_device(
    tokens,
    w_query,
    w_key,
    w_value,
    w_out,
    norm_gain,
    boundary,
    skip_offset,
    doc_lengths,
    batch_order,
):
    replicas, sections, groups = lax.axis_size("dp"), lax.axis_size("pipe"), lax.axis_size("tensor")
    my_replica, my_section, my_group = lax.axis_index("dp"), lax.axis_index("pipe"), lax.axis_index("tensor")
    micro_count, seq_len, local_width = tokens.shape
    model_width = local_width * groups
    slots = micro_count // sections
    rows = slots * seq_len
    depth = w_query.shape[2]
    q_heads = w_query.shape[3] // HEAD_DIM
    kv_heads = w_key.shape[3] // HEAD_DIM
    paired = replicas == groups and replicas & (replicas - 1) == 0

    spot = jnp.reshape(my_section, (1,)).astype(jnp.int32)
    parts = 2 if paired else 1
    part_len = seq_len // parts
    stream = pick_samples(tokens, batch_order, spot, slots, parts).reshape(rows, local_width)

    gain_rows = lax.dynamic_slice_in_dim(norm_gain, my_replica * depth, depth, 2)
    held = (w_query, w_key, w_value, w_out)
    if sections == 2:
        gain_traded = swapped(gain_rows, "pipe", 1)
        gain_traded, held = lax.optimization_barrier((gain_traded, held))
        held = (gain_rows, *held)
        traded = [gain_traded] + [swapped(w, "pipe", 1) for w in held[1:]]

        def layer_weights(index, section):
            return [
                jnp.where(my_section == section, mine[index, 0], theirs[index, 0])
                for mine, theirs in zip(held, traded)
            ]
    else:
        gathered = [lax.all_gather(w, "pipe", axis=1, tiled=True) for w in (gain_rows, *held)]

        def layer_weights(index, section):
            return [w[index, section] for w in gathered]

    turn = [(i * groups + j, j * groups + i) for i in range(replicas) for j in range(groups)]
    if paired:
        base = lax.bitwise_xor(my_replica, my_group)
        place = lax.bitwise_xor(jnp.asarray(partners("tensor", groups), jnp.int32), base)
        place_out = lax.rem(groups - lax.bitwise_xor(jnp.arange(replicas, dtype=jnp.int32), base), groups)
        blocks = gather_blocks(lax.ppermute(stream, ("dp", "tensor"), turn), "tensor", groups)
    else:
        place = place_out = jnp.zeros((1,), jnp.int32)
        wide = lax.all_gather(stream, "tensor", axis=1, tiled=True)
        blocks = [lax.all_to_all(wide, "dp", split_axis=1, concat_axis=0, tiled=True)]
    part_rows = slots * part_len
    total = replicas * part_rows

    layers = [(0, s) for s in range(sections)] + [(1, s) for s in reversed(range(sections))]
    weights = [layer_weights(*layer) for layer in layers]
    streams, sums, mixed, shares = ([None] * parts for _ in range(4))
    before = [[] for _ in layers]
    layout, latest, done = None, [], []

    def share_out(h, number):
        nonlocal layout, latest
        gain, wq, wk, wv, _ = weights[number]
        head, arrays, part = (streams[h], shares[h], None) if number else (place, blocks, h)
        streams[h], ends = project_qkv(
            head, arrays, part, total, gain[None], wq, wk, wv, replicas, latest
        )
        latest = [streams[h]]
        if layout is None:
            layout = layout_of(batch_order, boundary, skip_offset, doc_lengths, spot, slots, seq_len, ends[0])
        if paired:
            sums[h] = trade_blocks(ends, "dp")
        else:
            pieces = jnp.stack([end.astype(jnp.bfloat16) for end in ends])
            pieces = lax.all_to_all(pieces, "dp", split_axis=0, concat_axis=0)
            sums[h] = [jnp.sum(pieces.astype(jnp.float32), axis=0)]

    def mix(h, number):
        nonlocal latest
        rows_out, keys, values = attend(
            part_rows, sums[h], before[number], *layout, q_heads, kv_heads, model_width, latest
        )
        latest = [keys]
        before[number].append((keys, values))
        if paired:
            mixed[h] = gather_blocks(rows_out, "dp", replicas)
        else:
            mixed[h] = [lax.all_gather(rows_out, "dp", axis=0, tiled=True)]

    def bring_in(h, number):
        nonlocal latest
        last = number + 1 == len(layers)
        ends = project_out(
            mixed[h],
            place_out if paired and last else None,
            weights[number][4],
            groups if paired and last else 1,
            latest + done,
        )
        latest = ends[:1]
        if not paired:
            shares[h] = [lax.psum(ends[0].astype(jnp.float32), "tensor")]
        elif last:
            share = total_of(trade_blocks(ends, "tensor"))
            stream = lax.dynamic_slice_in_dim(streams[h], place[0] * part_rows, part_rows, 0)
            done.append((stream.astype(jnp.float32) + share).astype(jnp.bfloat16))
        else:
            shares[h] = gather_blocks(ends[0], "tensor", groups)

    for step, h, number in steps_of(parts, len(layers)):
        (share_out, mix, bring_in)[step](h, number)

    final = [lax.ppermute(stream, ("dp", "tensor"), turn) for stream in done]
    if not paired:
        for stream, share in zip(streams, shares):
            stream = (stream.astype(jnp.float32) + total_of(share)).astype(jnp.bfloat16)
            stream = lax.all_to_all(stream, "dp", split_axis=0, concat_axis=1, tiled=True)
            final.append(lax.dynamic_slice_in_dim(stream, my_group * local_width, local_width, 1))
    final = [stream.reshape(slots, part_len, local_width) for stream in final]
    if parts == sections == 2:
        first = my_section == 0
        came = swapped(jnp.where(first, final[1], final[0]), "pipe", 1)
        kept = jnp.where(first, final[0], final[1])
        return jnp.concatenate([jnp.where(first, kept, came), jnp.where(first, came, kept)], axis=0)
    final = jnp.concatenate(final, axis=1)
    return lax.all_to_all(final, "pipe", split_axis=1, concat_axis=0, tiled=True)


def solution(mesh):
    placed = (
        P("dp", None, "tensor"),
        P(None, "pipe", "dp", "tensor"),
        P(None, "pipe", "dp", "tensor"),
        P(None, "pipe", "dp", "tensor"),
        P(None, "pipe", "tensor", "dp"),
        P(None, "pipe", None),
        P("dp"),
        P("dp"),
        P("dp", None),
        P("dp", None),
    )
    return jax.shard_map(
        per_device, mesh=mesh, in_specs=placed, out_specs=P("dp", "pipe", "tensor"), check_vma=False
    )
```
